32 devices in a mesh: seq: 4 (over y, x), batch: 8 (over z, core).
Axes of the slice: x: 2, y: 2, z: 4, core: 2. Of those that a mesh axis runs over, the one named last changes fastest.
Arguments:
- tokens: bfloat16 [32, 1024, 512], P('batch', 'seq'), may hold values from -6 to 6
- lengths: int32 [32], P('batch'), may hold values from 513 to 1024, as said below
- query_weight: bfloat16 [512, 512], replicated, may hold values from -0.25 to 0.25
- key_weight: bfloat16 [512, 512], replicated, may hold values from -0.25 to 0.25
- value_weight: bfloat16 [512, 512], replicated, may hold values from -0.25 to 0.25
- output_weight: bfloat16 [512, 512], replicated, may hold values from -1 to 1
- up_weight: bfloat16 [512, 2048], replicated, may hold values from -0.25 to 0.25
- down_weight: bfloat16 [2048, 512], replicated, may hold values from -0.125 to 0.125
- query_bias: float32 [512], replicated, may hold values from -3 to 3
- value_bias: float32 [512], replicated, may hold values from -3 to 3
- output_bias: float32 [512], replicated, may hold values from -1.75 to 1.75
- up_bias: float32 [2048], replicated, may hold values from -3 to 3
- down_bias: float32 [512], replicated, may hold values from -1.75 to 1.75
- first_gain: float32 [512], replicated, may hold values from 0.25 to 1.75
- first_shift: float32 [512], replicated, may hold values from -1.75 to 1.75
- second_gain: float32 [512], replicated, may hold values from 0.25 to 1.75
- second_shift: float32 [512], replicated, may hold values from -1.75 to 1.75
- cotangent: bfloat16 [32, 1024, 512], P('batch', 'seq'), may hold values from -6 to 6
Outputs:
- layer_out: bfloat16 [32, 1024, 512], P('batch', 'seq')
- input_grad: float32 [32, 1024, 512], P('batch', 'seq')
- grad_query_weight: float32 [512, 512], replicated
- grad_key_weight: float32 [512, 512], replicated
- grad_value_weight: float32 [512, 512], replicated
- grad_output_weight: float32 [512, 512], replicated
- grad_up_weight: float32 [512, 2048], replicated
- grad_down_weight: float32 [2048, 512], replicated
- grad_query_bias: float32 [512], replicated
- grad_value_bias: float32 [512], replicated
- grad_output_bias: float32 [512], replicated
- grad_up_bias: float32 [2048], replicated
- grad_down_bias: float32 [512], replicated
- grad_first_gain: float32 [512], replicated
- grad_first_shift: float32 [512], replicated
- grad_second_gain: float32 [512], replicated
- grad_second_shift: float32 [512], replicated
The draws below stay inside these ranges and needn't reach their ends.
Inputs may be any that keep to these rules, and one draw needn't show every extreme that they name: `lengths`: among the 4 sequences held by one index of batch, one has length 1024.
All inputs are finite; a program needn't handle non-finite values.
Results may differ from the reference program's by a relative error of at most 0.02.
Values sent between devices are 32-bit elements; how exact they have to be, the bound alone decides.
No kernel may reach another device: no remote copies, remote signals or barrier semaphores. Data moves between devices by JAX's collectives and lax.ppermute only.
A program may use at most 256 MiB of HBM per device.

```python
import functools
import math
import jax
import jax.numpy as jnp
from jax import lax

D = 512
FF = 2048
HEADS = 8
HEAD_DIM = 64
BLOCK = 16
SEQ_DEV = 4
LEN = 1024
SEQUENCES = 32


def draw_lengths(key, part):
    key = jax.random.fold_in(key, 7)
    first_key, second_key = jax.random.split(key, 2)
    drawn = jax.random.randint(first_key, (SEQUENCES,), LEN // 2 + 1, LEN + 1)
    chosen = jax.random.randint(second_key, (SEQUENCES // SEQ_DEV,), 0, SEQ_DEV)
    within = jnp.arange(SEQUENCES, dtype=jnp.int32) % SEQ_DEV
    picked = jnp.repeat(chosen, SEQ_DEV)
    longest = within == picked
    shortest = within == (picked + 1) % SEQ_DEV
    return jnp.where(longest, LEN, jnp.where(shortest, LEN // 2 + 1, drawn)).astype(jnp.int32)


def level_of(key, shape, cuts, smallest, high):
    level, own = 1.0, jax.random.fold_in(key, 6)
    for position, shards_of in cuts:
        heights = jnp.exp(jax.random.uniform(jax.random.fold_in(own, position), (shards_of,), jnp.float32, smallest / len(cuts), high / len(cuts)))
        level = level * jnp.repeat(heights, shape[position] // shards_of).reshape([-1 if axis == position else 1 for axis in range(len(shape))])
    return level


def bell_draw(stream_key, shape, width, bound, pieces=(), held_as=jnp.bfloat16):
    entries = jax.random.normal(stream_key, shape, jnp.float32) * width
    if len(pieces) > 0:
        entries = level_of(stream_key, shape, pieces, -0.22, 0.18) * entries
    return jnp.clip(entries, min=-bound, max=bound).astype(held_as)


def setup_inputs(seed: int = 0) -> dict:
    splits = jax.random.split(jax.random.key(seed), 19)
    return {
        "tokens": bell_draw(splits[0], (SEQUENCES, LEN, D), 1.0, 6.0, ((0, 8), (1, 4))),
        "lengths": draw_lengths(jax.random.fold_in(splits[18], 71), 0),
        "query_weight": bell_draw(splits[2], (D, D), D ** -0.5, 0.25),
        "key_weight": bell_draw(splits[3], (D, D), D ** -0.5, 0.25),
        "value_weight": bell_draw(splits[4], (D, D), D ** -0.5, 0.25),
        "output_weight": bell_draw(splits[5], (D, D), (D // 16) ** -0.5, 1.0),
        "up_weight": bell_draw(splits[6], (D, FF), D ** -0.5, 0.25),
        "down_weight": bell_draw(splits[7], (FF, D), FF ** -0.5, 0.125),
        "query_bias": bell_draw(splits[8], (D,), 0.5, 3.0, (), jnp.float32),
        "value_bias": bell_draw(splits[9], (D,), 0.5, 3.0, (), jnp.float32),
        "output_bias": bell_draw(splits[10], (D,), 0.3, 1.75, (), jnp.float32),
        "up_bias": bell_draw(splits[11], (FF,), 0.5, 3.0, (), jnp.float32),
        "down_bias": bell_draw(splits[12], (D,), 0.3, 1.75, (), jnp.float32),
        "first_gain": jnp.clip(1.0 + 0.15 * jax.random.normal(splits[13], (D,), jnp.float32), 0.25, 1.75),
        "first_shift": bell_draw(splits[14], (D,), 0.3, 1.75, (), jnp.float32),
        "second_gain": jnp.clip(1.0 + 0.15 * jax.random.normal(splits[15], (D,), jnp.float32), 0.25, 1.75),
        "second_shift": bell_draw(splits[16], (D,), 0.3, 1.75, (), jnp.float32),
        "cotangent": bell_draw(splits[17], (SEQUENCES, LEN, D), 1.0, 6.0, ((0, 8), (1, 4))),
    }


@jax.custom_vjp
def low(v):
    return lax.optimization_barrier(v.astype(jnp.bfloat16)).astype(jnp.float32)

@jax.custom_vjp
def low_back(v):
    return v

def low_keep(v):
    return (low(v), None)

def low_pass(kept, grad):
    return (grad,)

def back_keep(v):
    return (v, None)

def back_low(kept, grad):
    return (low(grad),)
low.defvjp(low_keep, low_pass)
low_back.defvjp(back_keep, back_low)
HIGHEST = lax.Precision.HIGHEST
MASKED = -1e+30
EPSILON = 1e-05

def precise_dot(left, right):
    return jnp.dot(left, right, precision=HIGHEST)

def layer_norm(values, gain, shift):
    center = values - lax.optimization_barrier(jnp.mean(values, axis=-1, keepdims=True))
    variance = lax.optimization_barrier(jnp.mean(center * center, axis=-1, keepdims=True))
    return center * lax.rsqrt(variance + EPSILON) * gain + shift

def own_blocks(array):
    return array.reshape((array.shape[0] // BLOCK, BLOCK) + array.shape[1:])

def sibling_blocks(array):
    paired = array.reshape((array.shape[0] // (2 * BLOCK), 2, BLOCK) + array.shape[1:])
    return paired[:, ::-1].reshape((array.shape[0] // BLOCK, BLOCK) + array.shape[1:])

def hierarchy(queries, key_vectors, value_vectors, valid_mask):
    length = queries.shape[0]
    inverse_root = 1.0 / math.sqrt(HEAD_DIM)
    fine_bias = jnp.where(valid_mask > 0, 0.0, MASKED)
    near_keys = jnp.concatenate([own_blocks(key_vectors), sibling_blocks(key_vectors)], axis=1)
    near_values = jnp.concatenate([own_blocks(value_vectors), sibling_blocks(value_vectors)], axis=1)
    near_bias = jnp.concatenate([own_blocks(fine_bias), sibling_blocks(fine_bias)], axis=1)
    logits = jnp.einsum('bqhd,bkhd->bqhk', own_blocks(queries), near_keys, precision=HIGHEST) * inverse_root
    logits = low_back(logits + near_bias[:, None, None, :])
    maxima = lax.optimization_barrier(jnp.max(logits, axis=-1))
    powers = jnp.exp(logits - maxima[..., None])
    totals = lax.optimization_barrier(jnp.sum(powers, axis=-1))
    numerators = low_back(jnp.einsum('bqhk,bkhd->bqhd', low(powers), near_values, precision=HIGHEST))
    levels = [(maxima.reshape(length, HEADS), totals.reshape(length, HEADS), numerators.reshape(length, HEADS, HEAD_DIM))]
    factor = 2
    while length // factor >= 2 * BLOCK:
        coarse_count = length // factor
        pooled_queries = lax.optimization_barrier(jnp.mean(queries.reshape(coarse_count, factor, HEADS, HEAD_DIM), axis=1))
        counts = lax.optimization_barrier(jnp.sum(valid_mask.reshape(coarse_count, factor), axis=1))
        floored = jnp.maximum(counts, 1.0)
        masked_keys = key_vectors * valid_mask[:, None, None]
        masked_values = value_vectors * valid_mask[:, None, None]
        pooled_keys = lax.optimization_barrier(jnp.sum(masked_keys.reshape(coarse_count, factor, HEADS, HEAD_DIM), axis=1)) / floored[:, None, None]
        pooled_values = lax.optimization_barrier(jnp.sum(masked_values.reshape(coarse_count, factor, HEADS, HEAD_DIM), axis=1)) / floored[:, None, None]
        coarse_bias = jnp.where(counts > 0, jnp.log(floored), MASKED)
        logits = jnp.einsum('bqhd,bkhd->bqhk', own_blocks(pooled_queries), sibling_blocks(pooled_keys), precision=HIGHEST) * inverse_root
        logits = logits + sibling_blocks(coarse_bias)[:, None, None, :]
        maxima = lax.optimization_barrier(jnp.max(logits, axis=-1))
        powers = jnp.exp(logits - maxima[..., None])
        totals = lax.optimization_barrier(jnp.sum(powers, axis=-1))
        numerators = jnp.einsum('bqhk,bkhd->bqhd', powers, sibling_blocks(pooled_values), precision=HIGHEST)
        levels.append((jnp.repeat(maxima.reshape(coarse_count, HEADS), factor, axis=0), jnp.repeat(totals.reshape(coarse_count, HEADS), factor, axis=0), jnp.repeat(numerators.reshape(coarse_count, HEADS, HEAD_DIM), factor, axis=0)))
        factor = factor * 2
    biggest = functools.reduce(jnp.maximum, [record[0] for record in levels])
    denominator = functools.reduce(jnp.add, [jnp.exp(record[0] - biggest) * record[1] for record in levels])
    numerator = functools.reduce(jnp.add, [jnp.exp(record[0] - biggest)[..., None] * record[2] for record in levels])
    return numerator / denominator[..., None]

def block_layer(inputs, valid_mask, params):
    query_weight, key_weight, value_weight, output_weight, up_weight, down_weight, query_bias, value_bias, output_bias, up_bias, down_bias, first_gain, first_shift, second_gain, second_shift = params
    normed = low(layer_norm(inputs, first_gain, first_shift))
    queries = low(low_back(precise_dot(normed, query_weight) + query_bias))
    key_vectors = low(low_back(precise_dot(normed, key_weight)))
    value_vectors = low(low_back(precise_dot(normed, value_weight) + value_bias))
    head_shape = (inputs.shape[0], HEADS, HEAD_DIM)
    attended = hierarchy(queries.reshape(head_shape), key_vectors.reshape(head_shape), value_vectors.reshape(head_shape), valid_mask)
    attended = low(low_back(attended.reshape(inputs.shape)))
    middle = inputs + low_back(precise_dot(attended, output_weight) + output_bias)
    second = low(layer_norm(middle, second_gain, second_shift))
    hidden = low(jax.nn.gelu(low_back(precise_dot(second, up_weight) + up_bias), approximate=True))
    return middle + precise_dot(hidden, down_weight) + down_bias

def reference(tokens, lengths, query_weight, key_weight, value_weight, output_weight, up_weight, down_weight, query_bias, value_bias, output_bias, up_bias, down_bias, first_gain, first_shift, second_gain, second_shift, cotangent):
    params = tuple((weight.astype(jnp.float32) for weight in (query_weight, key_weight, value_weight, output_weight, up_weight, down_weight, query_bias, value_bias, output_bias, up_bias, down_bias, first_gain, first_shift, second_gain, second_shift)))
    group = math.gcd(SEQUENCES, max(1, 4096 // LEN))
    step_count = SEQUENCES // group
    grouped_inputs = tokens.astype(jnp.float32).reshape(step_count, group, LEN, D)
    grouped_lengths = lengths.reshape(step_count, group)
    grouped_cotangent = cotangent.astype(jnp.float32).reshape(step_count, group, LEN, D)
    positions = jnp.arange(LEN)

    def advance(carry, record):
        block_inputs, block_lengths, block_cotangent = record
        masks = (positions[None, :] < block_lengths[:, None]).astype(jnp.float32)

        def forward(values, weights):
            return jax.vmap(block_layer, in_axes=(0, 0, None))(values, masks, weights)
        outputs, pullback = jax.vjp(forward, block_inputs, params)
        grad_inputs, grad_weights = pullback(block_cotangent)
        carry = jax.tree.map(jnp.add, carry, grad_weights)
        return (carry, (outputs.astype(jnp.bfloat16), grad_inputs))
    zeros = tuple((jnp.zeros_like(weight) for weight in params))
    summed, (outputs, grad_inputs) = lax.scan(advance, zeros, (grouped_inputs, grouped_lengths, grouped_cotangent))
    return (outputs.reshape(SEQUENCES, LEN, D), grad_inputs.reshape(SEQUENCES, LEN, D), summed[0], summed[1], summed[2], summed[3], summed[4], summed[5], summed[6], summed[7], summed[8], summed[9], summed[10], summed[11], summed[12], summed[13], summed[14])
```

```python
import functools

import jax
import jax.numpy as jnp
import numpy as np
from jax import lax
from jax.experimental import pallas as pl
from jax.experimental.pallas import tpu as pltpu
from jax.sharding import PartitionSpec as P

HEADS = 8
BLOCK = 16
CHUNK = 128
PAIR = 128
HALF = 64
LOCAL_ROWS = (128, 64, 32, 16)
LOCAL_STARTS = (0, 128, 192, 224)
LOCAL_KEYS = 240
COARSE_KEYS = 112
MASKED = -1e30
TOKEN = (8, 128)
ROUND_BYTES = dict(down=40_000_000, up=40_000_000, last=40_000_000)
ROUNDS = "u,d,ud,dudldluudlldulduluoludluldlul"
TILE = 32
EPSILON = 1e-05
VMEM_BYTES = 62 * 2**20
F32 = jnp.float32
BF16 = jnp.bfloat16


def dot(left, right):
    return lax.dot_general(left, right, (((1,), (0,)), ((), ())), preferred_element_type=F32)


def dot_nt(left, right):
    return lax.dot_general(left, right, (((1,), (1,)), ((), ())), preferred_element_type=F32)


def dot_tn(left, right):
    return lax.dot_general(left, right, (((0,), (0,)), ((), ())), preferred_element_type=F32)


def iota(shape, axis):
    return lax.broadcasted_iota(jnp.int32, shape, axis)


def row_mean(values):
    return jnp.mean(values, axis=-1, keepdims=True)


def column_sum(values):
    return jnp.sum(values, axis=0, keepdims=True)


def normalize(values):
    center = values - row_mean(values)
    scale = lax.rsqrt(row_mean(center * center) + EPSILON)
    return center * scale, scale


def normalize_back(grads, normed, scale):
    return scale * (grads - row_mean(grads) - normed * row_mean(grads * normed))


def block_diagonal(block):
    zeros = jnp.zeros((HALF, CHUNK), block.dtype)
    first = jnp.concatenate([block[:HALF], zeros], axis=1)
    second = jnp.concatenate([zeros, block[HALF:]], axis=1)
    return jnp.concatenate([first, second], axis=0)


def diagonal_blocks(wide):
    return jnp.concatenate([wide[:HALF, :CHUNK], wide[HALF:, CHUNK:]], axis=0)


def head_rows(row):
    first = jnp.broadcast_to(row[:, :CHUNK], (HALF, CHUNK))
    second = jnp.broadcast_to(row[:, CHUNK:], (HALF, CHUNK))
    return jnp.concatenate([first, second], axis=0)


def twice(block):
    return jnp.concatenate([block, block], axis=1)


def four_times(block):
    return jnp.concatenate([block, block, block, block], axis=1)


def averaging(level):
    spots = np.arange(CHUNK) >> level
    return (spots[:, None] == spots[None, :]).astype(np.float32) / (1 << level)


def averaging_pair(level):
    return np.kron(np.eye(2, dtype=np.float32), averaging(level))


def coarse_members(tok_count):
    spots = np.arange(tok_count)
    rows = []
    for chunk in range(2):
        for level in range(1, 4):
            first = (chunk if level < 3 else 1 - chunk) * CHUNK
            begins = first + (np.arange(LOCAL_ROWS[level]) << level)
            inside = spots[None, :] - begins[:, None]
            rows.append((inside >= 0) & (inside < (1 << level)))
    return np.concatenate(rows, axis=0).astype(np.float32)


def group_members(tok_count, factor):
    spots = np.arange(tok_count) // factor
    return (np.arange(tok_count // factor)[:, None] == spots[None, :]).astype(np.float32)


def local_counts(remaining, chunk, level):
    rows = LOCAL_ROWS[level]
    spots = iota((rows, CHUNK), 0) << level
    first = (chunk if level < 3 else 1 - chunk) * CHUNK
    return jnp.clip(remaining - (first + spots), 0, 1 << level), spots


def local_bias(remaining, chunk):
    parts = []
    for level in range(4):
        counts, spots = local_counts(remaining, chunk, level)
        allowed = counts > 0
        places = iota(counts.shape, 1)
        if level == 0:
            allowed = allowed & ((spots >> 5) == (places >> 5))
        elif level < 3:
            allowed = allowed & (((spots >> (4 + level)) ^ (places >> (4 + level))) == 1)
        logs = jnp.log(jnp.maximum(counts, 1).astype(F32))
        parts.append(jnp.where(allowed, logs, MASKED))
    return parts


def coarse_inverse(remaining):
    parts = []
    for chunk in range(2):
        for level in range(1, 4):
            counts, _ = local_counts(remaining, chunk, level)
            parts.append(1.0 / jnp.maximum(counts, 1).astype(F32))
    return jnp.concatenate(parts, axis=0)


def pooled_keys(members, rows, inverse):
    return (dot(members, rows) * four_times(inverse)).astype(BF16)


def chunk_keys(rows, pooled):
    return [
        jnp.concatenate(
            [
                rows[chunk * CHUNK : (chunk + 1) * CHUNK],
                pooled[chunk * COARSE_KEYS : (chunk + 1) * COARSE_KEYS],
            ],
            axis=0,
        )
        for chunk in range(2)
    ]


def level_queries(queries, coarse, chunk):
    levels = coarse.shape[1] // CHUNK // 2
    parts = [queries[:, chunk * CHUNK : (chunk + 1) * CHUNK]]
    for at in range(chunk * levels, (chunk + 1) * levels):
        parts.append(coarse[:, at * CHUNK : (at + 1) * CHUNK])
    return parts


UNITS = [(chunk, pair) for chunk in range(2) for pair in range(HEADS // 2)]


def skewed(first, *stages):
    held = {}
    for tick in range(len(UNITS) + len(stages)):
        for stage in range(len(stages) + 1):
            at = tick - stage
            if 0 <= at < len(UNITS):
                unit = UNITS[at]
                if stage == 0:
                    held[unit] = first(unit)
                else:
                    held[unit] = stages[stage - 1](unit, held[unit])
    return held


def interleaved(work, count):
    runs = [work(at) for at in range(count)]
    while runs:
        runs = [run for run in runs if next(run, run) is not run]


def pair_of(index):
    return slice(index * PAIR, (index + 1) * PAIR)


def local_logits(keys, tall, pair):
    return [
        dot(
            keys[LOCAL_STARTS[level] : LOCAL_STARTS[level] + LOCAL_ROWS[level], pair_of(pair)],
            tall[level],
        )
        for level in range(4)
    ]


def tiles(rows, size=TILE):
    return [slice(begin, begin + size) for begin in range(0, rows, size)]


def partial_sum(values):
    return jnp.sum(values.reshape(-1, 8, values.shape[1]), axis=0)


def add_to(ref, values):
    for rows in tiles(values.shape[0]):
        ref[rows, :] += values[rows]


def project_kernel(
    heights,
    lengths_ref,
    shard_ref,
    tokens_ref,
    query_weight_ref,
    key_weight_ref,
    value_weight_ref,
    query_bias_ref,
    value_bias_ref,
    gain_ref,
    shift_ref,
    groups_ref,
    queries_ref,
    keys_ref,
    values_ref,
    *refs,
):
    sums_refs, normed_ref, turned_ref = refs[:heights], refs[heights], refs[heights + 1]
    count, tok_count, width = tokens_ref.shape
    gain, shift = gain_ref[...], shift_ref[...]
    for at in range(count):
        for rows in tiles(tok_count):
            normed, _ = normalize(tokens_ref[at, rows].astype(F32))
            normed_ref[at, rows] = (normed * gain + shift).astype(BF16)
    normed = normed_ref[...].reshape(count * tok_count, width)
    keys_wide = dot(normed, key_weight_ref[...])
    values_wide = dot(normed, value_weight_ref[...])
    queries_wide = dot(normed, query_weight_ref[...])
    value_bias, query_bias = value_bias_ref[...], query_bias_ref[...]
    for at in range(count):
        remaining = lengths_ref[pl.program_id(0) * count + at] - shard_ref[0] * tok_count
        for rows in tiles(tok_count):
            places = slice(at * tok_count + rows.start, at * tok_count + rows.stop)
            valid = iota((TILE, width), 0) + rows.start < remaining
            keys_ref[at, rows] = jnp.where(valid, keys_wide[places], 0.0).astype(BF16)
            values = values_wide[places] + value_bias
            values_ref[at, rows] = jnp.where(valid, values, 0.0).astype(BF16)
            turned_ref[at, rows] = ((queries_wide[places] + query_bias) * 0.125).astype(BF16)
        key_sums = dot(groups_ref[...], keys_ref[at])
        value_sums = dot(groups_ref[...], values_ref[at])
        begin = 0
        for height in range(heights):
            size = BLOCK >> height
            sums_refs[height][at, :, :width] = key_sums[begin : begin + size]
            sums_refs[height][at, :, width:] = value_sums[begin : begin + size]
            begin += max(size, 8)
        queries_ref[at] = turned_ref[at].T


def near_kernel(
    lengths_ref,
    shard_ref,
    queries_ref,
    keys_ref,
    values_ref,
    members_ref,
    spread_ref,
    maxima_ref,
    totals_ref,
    numer_ref,
    coarse_ref,
    pooled_keys_ref,
    pooled_values_ref,
):
    sequence = pl.program_id(0)
    tok_count = keys_ref.shape[1]
    remaining = lengths_ref[sequence] - shard_ref[0] * tok_count
    inverse = coarse_inverse(remaining)
    pooled_keys_ref[0] = pooled_keys(members_ref[...], keys_ref[0], inverse)
    pooled_values_ref[0] = pooled_keys(members_ref[...], values_ref[0], inverse)
    keys = chunk_keys(keys_ref[0], pooled_keys_ref[0])
    values = chunk_keys(values_ref[0], pooled_values_ref[0])
    queries = queries_ref[0]
    bias = [local_bias(remaining, chunk) for chunk in range(2)]
    columns = spread_ref.shape[1]
    for chunk in range(2):
        own = queries[:, chunk * CHUNK : (chunk + 1) * CHUNK]
        coarse_ref[0, :, chunk * columns : (chunk + 1) * columns] = dot(
            own, spread_ref[...]
        ).astype(BF16)
    coarse = coarse_ref[0]
    levels = [level_queries(queries, coarse, chunk) for chunk in range(2)]

    def logits_of(unit):
        chunk, pair = unit
        tall = [block_diagonal(part[pair_of(pair)]) for part in levels[chunk]]
        return local_logits(keys[chunk], tall, pair)

    def softmax_of(unit, logits):
        chunk, pair = unit
        lanes = slice(chunk * CHUNK, (chunk + 1) * CHUNK)
        both = []
        for side in range(2):
            half = slice(side * CHUNK, (side + 1) * CHUNK)
            head = 2 * pair + side
            parts = [part[:, half] + extra for part, extra in zip(logits, bias[chunk])]
            maxima = functools.reduce(
                jnp.maximum, [jnp.max(part, axis=0, keepdims=True) for part in parts]
            )
            parts = [jnp.exp(part - maxima) for part in parts]
            maxima_ref[0, head : head + 1, lanes] = maxima
            totals = sum(partial_sum(part) for part in parts)
            totals_ref[0, head : head + 1, lanes] = column_sum(totals)
            both.append(jnp.concatenate([part.astype(BF16) for part in parts], axis=0))
        return jnp.concatenate(both, axis=1)

    def numer_of(unit, powers):
        chunk, pair = unit
        lanes = slice(chunk * CHUNK, (chunk + 1) * CHUNK)
        wide = dot_tn(values[chunk][:, pair_of(pair)], powers)
        numer_ref[0, pair_of(pair), lanes] = diagonal_blocks(wide).astype(BF16)

    skewed(logits_of, softmax_of, numer_of)


def split_rows(source_ref, core, send_ref, keep_ref):
    rows = send_ref.shape[0]
    send_ref[...] = source_ref[pl.ds(pl.multiple_of((1 - core) * rows, 8), rows), :]
    keep_ref[...] = source_ref[pl.ds(pl.multiple_of(core * rows, 8), rows), :]


def far_counts(length, shard, tok_count, heights, shards):
    spots = iota((BLOCK * heights, CHUNK), 0)
    begins = jnp.zeros_like(spots)
    widths = jnp.ones_like(spots)
    row = 0
    for mask in range(1, shards):
        height = mask.bit_length() - 1
        rows = BLOCK >> height
        inside = (spots >= row) & (spots < row + rows)
        first = jnp.bitwise_xor(shard, mask) * tok_count
        begins = jnp.where(inside, first + ((spots - row) << (4 + height)), begins)
        widths = jnp.where(inside, BLOCK << height, widths)
        row += rows
    return jnp.minimum(jnp.maximum(length - begins, 0), widths)


def half_lanes(shape, side):
    return iota(shape, 1) // HALF == side


def by_head(rows):
    blocks = []
    for head in range(HEADS):
        parts = [jnp.zeros((BLOCK, PAIR), F32)] * (HEADS // 2)
        part = rows[:, pair_of(head // 2)]
        parts[head // 2] = jnp.where(half_lanes(part.shape, head % 2), part, 0.0)
        blocks.append(jnp.concatenate(parts, axis=1))
    return jnp.concatenate(blocks, axis=0).astype(BF16)


def of_heads(wide):
    parts = []
    for pair in range(HEADS // 2):
        first = wide[2 * pair * BLOCK : (2 * pair + 1) * BLOCK, pair_of(pair)]
        second = wide[(2 * pair + 1) * BLOCK : (2 * pair + 2) * BLOCK, pair_of(pair)]
        parts.append(jnp.where(half_lanes(first.shape, 0), first, second))
    return jnp.concatenate(parts, axis=1)


def far_state(sequence, lengths_ref, shard, tok_count, heights, shards, pieces):
    counts = far_counts(lengths_ref[sequence], shard, tok_count, heights, shards)
    floored = jnp.maximum(counts, 1).astype(F32)
    inverse = four_times(1.0 / floored)
    bias = twice(jnp.where(counts > 0, jnp.log(floored), MASKED))
    bias = [bias[BLOCK * at : BLOCK * (at + 1)] for at in range(heights)]
    sums = jnp.concatenate([piece[sequence] for piece in pieces], axis=0)
    width = sums.shape[1] // 2
    keys, values = [], []
    for at in range(heights):
        rows = slice(BLOCK * at, BLOCK * (at + 1))
        keys.append(by_head(sums[rows, :width] * inverse[rows]))
        values.append(by_head(sums[rows, width:] * inverse[rows]))
    return keys, jnp.concatenate(values, axis=0), bias, inverse


def far_queries_of(queries, spread_ref, heights):
    return [dot(queries, spread_ref[at]).astype(BF16) for at in range(heights)]


def join_kernel(
    heights,
    shards,
    piece_count,
    lengths_ref,
    shard_ref,
    tokens_ref,
    queries_ref,
    maxima_ref,
    totals_ref,
    numer_ref,
    output_weight_ref,
    output_bias_ref,
    gain_ref,
    shift_ref,
    spread_ref,
    *refs,
):
    pieces = refs[:piece_count]
    middle_ref, second_ref, outs_ref, level_ref, far_ref, attended_ref = refs[piece_count:]
    count, tok_count, _ = tokens_ref.shape
    bias, gain, shift = output_bias_ref[...], gain_ref[...], shift_ref[...]

    def work(own):
        far_keys, far_values, far_bias, _ = far_state(
            pl.program_id(0) * count + own, lengths_ref, shard_ref[0], tok_count, heights, shards, pieces
        )
        coarse = far_queries_of(queries_ref[own], spread_ref, heights)
        for at in range(heights):
            far_ref[own, :, at * tok_count : (at + 1) * tok_count] = coarse[at]
        logits = [dot(far_keys[at], coarse[at]) for at in range(heights)]
        yield
        powers = [[] for _ in range(heights)]
        fades, inverses = [], []
        for head in range(HEADS):
            rows = slice(BLOCK * head, BLOCK * (head + 1))
            near_maxima = maxima_ref[own, head : head + 1, :]
            parts = [logits[at][rows] + far_bias[at] for at in range(heights)]
            maxima = functools.reduce(jnp.maximum, parts)
            maxima = jnp.maximum(near_maxima, jnp.max(maxima, axis=0, keepdims=True))
            fade = jnp.exp(near_maxima - maxima)
            parts = [jnp.exp(part - maxima) for part in parts]
            totals = fade * totals_ref[own, head : head + 1, :] + column_sum(sum(parts))
            for at in range(heights):
                powers[at].append(parts[at].astype(BF16))
            level_ref[own, head : head + 1, :] = maxima + jnp.log(totals)
            inverse = 1.0 / totals
            fades.append(fade * inverse)
            inverses.append(inverse)
        yield
        far_numer = dot_tn(far_values, jnp.concatenate(sum(powers, []), axis=0))
        yield
        for head in range(HEADS):
            rows = slice(HALF * head, HALF * (head + 1))
            outs = numer_ref[own, rows, :].astype(F32) * fades[head] + far_numer[rows] * inverses[head]
            outs_ref[own, rows, :] = outs
            attended_ref[own, rows, :] = outs.astype(BF16)
        yield
        projected = dot_tn(attended_ref[own], output_weight_ref[...])
        yield
        for rows in tiles(tok_count):
            middle = tokens_ref[own, rows].astype(F32) + projected[rows] + bias
            middle_ref[own, rows] = middle
            normed, _ = normalize(middle)
            second_ref[own, rows] = (normed * gain + shift).astype(BF16)

    interleaved(work, count)


def hidden_kernel(
    step_count,
    core_ref,
    second_ref,
    cotangent_ref,
    up_weight_ref,
    down_weight_ref,
    up_bias_ref,
    grad_second_ref,
    down_send_ref,
    down_keep_ref,
    up_send_ref,
    up_keep_ref,
    bias_ref,
    hidden_ref,
    total_ref,
    second_turned_ref,
    grad_hidden_ref,
):
    step = pl.program_id(0)
    seq_count, tok_count, width = second_ref.shape

    @pl.when(step == 0)
    def _():
        total_ref[...] = jnp.zeros_like(total_ref)
        for at in range(seq_count):
            second_turned_ref[:, at * tok_count : (at + 1) * tok_count] = second_ref[at].T

    up_weight, down_weight = up_weight_ref[...], down_weight_ref[...]

    together = 2 - seq_count % 2
    block = together * tok_count

    def flat(ref, at):
        return ref[at * together : (at + 1) * together].reshape(block, width)

    def products(at):
        return (
            dot(flat(second_ref, at), up_weight),
            dot_nt(flat(cotangent_ref, at), down_weight),
        )

    up_bias = up_bias_ref[...]

    def bend(at, state):
        bias = 0.0
        for rows in tiles(block, TILE // 2):
            hidden_in = state[0][rows] + up_bias
            squares = hidden_in * hidden_in
            bent = jnp.tanh(hidden_in * (0.7978845608028654 + 0.035677408136300125 * squares))
            rising = 0.5 + 0.5 * bent
            slope = rising + hidden_in * (0.5 - 0.5 * bent * bent) * (
                0.7978845608028654 + 0.10703222440890037 * squares
            )
            grad_hidden = (state[1][rows] * slope).astype(BF16)
            places = slice(at * block + rows.start, at * block + rows.stop)
            hidden_ref[places, :] = (hidden_in * rising).astype(BF16)
            grad_hidden_ref[places, :] = grad_hidden
            bias = bias + partial_sum(grad_hidden.astype(F32))
        return bias

    def spread(at):
        rows = slice(at * block, (at + 1) * block)
        grads = dot_nt(grad_hidden_ref[rows, :], up_weight)
        for rows in tiles(block):
            sequence = at * together + rows.start // tok_count
            begin = rows.start % tok_count
            places = slice(begin, begin + TILE)
            total_ref[sequence, places] += grads[rows]

    state = products(0)
    bias = 0.0
    for at in range(seq_count // together):
        later = products(at + 1) if at + 1 < seq_count // together else None
        bias = bias + bend(at, state)
        spread(at)
        state = later
    bias_ref[...] = column_sum(bias)
    down = dot_tn(hidden_ref[...], cotangent_ref[...].reshape(seq_count * tok_count, width))
    up = dot(second_turned_ref[...], grad_hidden_ref[...]).reshape(up_send_ref.shape)

    @pl.when(step < step_count // 2)
    def _():
        down_send_ref[0] = down
        up_send_ref[...] = up

    @pl.when(step >= step_count // 2)
    def _():
        down_keep_ref[0] = down
        up_keep_ref[...] = up

    @pl.when(step == step_count - 1)
    def _():
        for at in range(seq_count):
            for rows in tiles(tok_count):
                grad_second_ref[at, rows] = total_ref[at, rows].astype(BF16)


def output_kernel(
    core_ref, hidden_ref, middle_ref, down_weight_ref, down_bias_ref, layer_ref
):
    results = dot(hidden_ref[...], down_weight_ref[...])
    bias = down_bias_ref[...]
    for rows in tiles(results.shape[0]):
        layer_ref[0, rows] = (middle_ref[0, rows] + results[rows] + bias).astype(BF16)


def backward_kernel(
    heights,
    shards,
    piece_count,
    lengths_ref,
    shard_ref,
    cotangent_ref,
    far_ref,
    middle_ref,
    outs_ref,
    level_ref,
    grad_second_ref,
    output_weight_ref,
    gain_ref,
    spread_ref,
    *refs,
):
    pieces = refs[:piece_count]
    refs = refs[piece_count + 2 :]
    grad_middle_ref, grad_attended_ref, inner_ref, grad_queries_ref = refs[:4]
    grad_pieces = refs[4 : piece_count + 4]
    send_ref, keep_ref, small_ref, weights_ref, project_ref, attended_ref = refs[piece_count + 4 :]
    step = pl.program_id(0)
    count, tok_count, width = middle_ref.shape

    @pl.when(step == 0)
    def _():
        weights_ref[...] = jnp.zeros_like(weights_ref)
        small_ref[...] = jnp.zeros_like(small_ref)

    gain = gain_ref[...]

    def work(own):
        far_keys, far_values, far_bias, inverse = far_state(
            step * count + own, lengths_ref, shard_ref[0], tok_count, heights, shards, pieces
        )
        coarse = [far_ref[own, :, at * tok_count : (at + 1) * tok_count] for at in range(heights)]
        logits = [dot(far_keys[at], coarse[at]) for at in range(heights)]
        yield
        small = [0.0] * 4
        for rows in tiles(tok_count):
            normed, scale = normalize(middle_ref[own, rows])
            grad_second = grad_second_ref[own, rows].astype(F32)
            grad_result = cotangent_ref[own, rows].astype(F32)
            grad_middle = grad_result + normalize_back(grad_second * gain, normed, scale)
            grad_middle_ref[own, rows] = grad_middle
            grad_project = grad_middle.astype(BF16)
            project_ref[own, rows] = grad_project
            sums = [grad_result, grad_second * normed, grad_second, grad_project.astype(F32)]
            small = [total + partial_sum(part) for total, part in zip(small, sums)]
        for at, total in enumerate(small):
            small_ref[:, at * width : (at + 1) * width] += column_sum(total)
        grad_project = project_ref[own]
        yield
        grad_attended = dot_nt(output_weight_ref[...], grad_project)
        yield
        inners = []
        for head in range(HEADS):
            rows = slice(HALF * head, HALF * (head + 1))
            outs = outs_ref[own, rows, :]
            attended_ref[own, rows, :] = outs.astype(BF16)
            grads = grad_attended[rows].astype(BF16)
            grad_attended_ref[own, rows, :] = grads
            inners.append(column_sum(partial_sum(grads.astype(F32) * outs)))
            inner_ref[own, head : head + 1, :] = inners[-1]
        yield
        grad_attended = grad_attended_ref[own]
        add_to(weights_ref, dot(attended_ref[own], grad_project))
        grad_probs = dot(far_values, grad_attended)
        yield
        all_probs, all_grads = [], []
        for at in range(heights):
            probs_parts, grads_parts = [], []
            for head in range(HEADS):
                rows = slice(BLOCK * head, BLOCK * (head + 1))
                whole_rows = slice(HEADS * BLOCK * at + rows.start, HEADS * BLOCK * at + rows.stop)
                level = level_ref[own, head : head + 1, :]
                probs = jnp.exp(logits[at][rows] + far_bias[at] - level)
                probs_parts.append(probs.astype(BF16))
                grads_parts.append((probs * (grad_probs[whole_rows] - inners[head])).astype(BF16))
            all_probs.append(jnp.concatenate(probs_parts, axis=0))
            all_grads.append(jnp.concatenate(grads_parts, axis=0))
        yield
        all_spread = [dot(all_grads[at], spread_ref[at]).astype(BF16) for at in range(heights)]
        yield
        grad_queries = dot_tn(jnp.concatenate(far_keys, axis=0), jnp.concatenate(all_spread, axis=0))
        grad_queries_ref[own] = grad_queries.astype(BF16)
        wide_values = dot_nt(jnp.concatenate(all_probs, axis=0), grad_attended)
        yield
        grad_keys, grad_values = [], []
        for at in range(heights):
            rows = slice(HEADS * BLOCK * at, HEADS * BLOCK * (at + 1))
            grad_keys.append(of_heads(dot_nt(all_grads[at], coarse[at])))
            grad_values.append(of_heads(wide_values[rows]))
        grad_sums = jnp.concatenate(
            [
                jnp.concatenate(grad_keys, axis=0) * inverse,
                jnp.concatenate(grad_values, axis=0) * inverse,
            ],
            axis=1,
        )
        row = 0
        for piece in grad_pieces:
            rows = piece.shape[1]
            piece[own] = grad_sums[row : row + rows]
            row += rows

    interleaved(work, count)

    @pl.when(step == pl.num_programs(0) - 1)
    def _():
        split_rows(weights_ref, shard_ref[1], send_ref.at[0], keep_ref.at[0])


def near_back_kernel(
    begin,
    summing,
    lengths_ref,
    shard_ref,
    bits_ref,
    queries_ref,
    keys_ref,
    values_ref,
    grad_attended_ref,
    level_ref,
    inner_ref,
    spots_ref,
    spread_pair_ref,
    far_queries_ref,
    coarse_ref,
    pooled_keys_ref,
    pooled_values_ref,
    *refs,
):
    grad_queries_ref, grad_keys_ref, grad_values_ref, send_ref = refs[-4:]
    if summing:
        keep_ref, other_ref = refs[-6:-4]
        send_ref[...] = keep_ref[...] + other_ref[...]
    sequence = pl.program_id(0) + begin
    tok_count = keys_ref.shape[1]
    remaining = lengths_ref[sequence] - shard_ref[0] * tok_count
    inverse = coarse_inverse(remaining)
    keys = chunk_keys(keys_ref[0], pooled_keys_ref[0])
    values = chunk_keys(values_ref[0], pooled_values_ref[0])
    queries = queries_ref[0]
    grad_attended = grad_attended_ref[0]
    bias = [local_bias(remaining, chunk) for chunk in range(2)]
    coarse = coarse_ref[0]
    levels = [level_queries(queries, coarse, chunk) for chunk in range(2)]
    grad_keys, grad_values = {}, {}

    def products(unit):
        chunk, pair = unit
        lanes = slice(chunk * CHUNK, (chunk + 1) * CHUNK)
        tall = [block_diagonal(part[pair_of(pair)]) for part in levels[chunk]]
        tall_grads = block_diagonal(grad_attended[pair_of(pair), lanes])
        logits = local_logits(keys[chunk], tall, pair)
        return tall[0], tall_grads, logits, dot(values[chunk][:, pair_of(pair)], tall_grads)

    def slopes(unit, state):
        chunk, pair = unit
        lanes = slice(chunk * CHUNK, (chunk + 1) * CHUNK)
        tall, tall_grads, logits, grad_probs = state
        probs_sides, grads_sides = [], []
        for side in range(2):
            half = slice(side * CHUNK, (side + 1) * CHUNK)
            head = 2 * pair + side
            level = level_ref[0, head : head + 1, lanes]
            inner = inner_ref[0, head : head + 1, lanes]
            probs_parts, grads_parts = [], []
            for at in range(4):
                for rows in tiles(LOCAL_ROWS[at], min(LOCAL_ROWS[at], 2 * TILE)):
                    begin = LOCAL_STARTS[at] + rows.start
                    probs = jnp.exp(logits[at][rows, half] + bias[chunk][at][rows] - level)
                    grads = grad_probs[begin : begin + rows.stop - rows.start, half]
                    probs_parts.append(probs.astype(BF16))
                    grads_parts.append((probs * (grads - inner)).astype(BF16))
            probs_sides.append(jnp.concatenate(probs_parts, axis=0))
            grads_sides.append(jnp.concatenate(grads_parts, axis=0))
        return (
            tall,
            tall_grads,
            jnp.concatenate(probs_sides, axis=1),
            jnp.concatenate(grads_sides, axis=1),
        )

    def grads(unit, state):
        tall, tall_grads, probs, grad_logits = state
        grad_values[unit] = dot_nt(probs, tall_grads)
        return tall, grad_logits

    held = skewed(products, slopes, grads)
    for chunk in range(2):
        lanes = slice(chunk * CHUNK, (chunk + 1) * CHUNK)
        pairs = range(HEADS // 2)
        spread = []
        for at in range(1, 4):
            begin, rows = LOCAL_STARTS[at], LOCAL_ROWS[at]
            parts = [held[chunk, pair][1][begin : begin + rows] for pair in pairs]
            spread.append(
                dot(jnp.concatenate(parts, axis=0), spread_pair_ref[at - 1]).astype(BF16)
            )
        for pair in pairs:
            tall, grad_logits = held[chunk, pair]
            parts = [grad_logits[:CHUNK]] + [
                spread[at - 1][pair * LOCAL_ROWS[at] : (pair + 1) * LOCAL_ROWS[at]]
                for at in range(1, 4)
            ]
            evened = jnp.concatenate(parts, axis=0)
            grad_keys[chunk, pair] = dot_nt(evened, tall)
            wide = dot_tn(keys[chunk][:, pair_of(pair)], evened)
            total = diagonal_blocks(wide) + far_queries_ref[0, pair_of(pair), lanes].astype(F32)
            grad_queries_ref[0, pair_of(pair), lanes] = (total * 0.125).astype(BF16)

    def gathered(parts, begin, end):
        return [
            jnp.concatenate([parts[chunk, pair][begin:end] for pair in range(HEADS // 2)], axis=1)
            for chunk in range(2)
        ]

    fine_keys, coarse_keys = gathered(grad_keys, 0, CHUNK), gathered(grad_keys, CHUNK, LOCAL_KEYS)
    fine_values = gathered(grad_values, 0, CHUNK)
    coarse_values = gathered(grad_values, CHUNK, LOCAL_KEYS)
    inverse = four_times(inverse)
    for out_ref, fine, coarse in (
        (grad_keys_ref, fine_keys, coarse_keys),
        (grad_values_ref, fine_values, coarse_values),
    ):
        pooled = (jnp.concatenate(coarse, axis=0) * inverse).astype(BF16)
        total = jnp.concatenate(fine, axis=0) + dot(spots_ref[...], pooled)
        out_ref[0] = total.astype(out_ref.dtype)


def last_kernel(
    heights,
    piece_heights,
    lengths_ref,
    shard_ref,
    tokens_ref,
    grad_middle_ref,
    grad_queries_ref,
    grad_keys_ref,
    grad_values_ref,
    query_weight_ref,
    key_weight_ref,
    value_weight_ref,
    gain_ref,
    shift_ref,
    groups_ref,
    grad_up_bias_ref,
    small_middle_ref,
    *refs,
):
    pieces = refs[: len(piece_heights)]
    input_grad_ref, send_ref, keep_ref, weights_ref, small_ref, normed_ref, grads_ref = refs[-7:]
    sequence = pl.program_id(0)
    count, tok_count, width = tokens_ref.shape

    @pl.when(sequence == 0)
    def _():
        weights_ref[...] = jnp.zeros_like(weights_ref)
        small_ref[0:1, :] = grad_up_bias_ref[...]
        small_ref[1:2, :] = small_middle_ref[...]
        small_ref[2:, :] = jnp.zeros((small_ref.shape[0] - 2, small_ref.shape[1]), F32)

    gain, shift = gain_ref[...], shift_ref[...]
    for at in range(count):
        remaining = lengths_ref[sequence * count + at] - shard_ref[0] * tok_count
        far = [
            sum(piece[at] for piece, level in zip(pieces, piece_heights) if level == height)
            for height in range(heights)
        ]
        far = dot_tn(groups_ref[...], jnp.concatenate(far, axis=0).astype(BF16))
        grads_ref[at, :, :width] = grad_queries_ref[at].T
        for rows in tiles(tok_count):
            normed, _ = normalize(tokens_ref[at, rows].astype(F32))
            normed_ref[at, rows] = (normed * gain + shift).astype(BF16)
            valid = iota((TILE, width), 0) + rows.start < remaining
            keys = grad_keys_ref[at, rows].astype(F32) + far[rows, :width]
            values = grad_values_ref[at, rows].astype(F32) + far[rows, width:]
            keys = jnp.where(valid, keys, 0.0)
            values = jnp.where(valid, values, 0.0)
            grads_ref[at, rows, width : 2 * width] = keys.astype(BF16)
            grads_ref[at, rows, 2 * width :] = values.astype(BF16)
    grads = grads_ref[...].reshape(count * tok_count, 3 * width)
    grad_normed = (
        dot_nt(grads[:, :width], query_weight_ref[...])
        + dot_nt(grads[:, width : 2 * width], key_weight_ref[...])
        + dot_nt(grads[:, 2 * width :], value_weight_ref[...])
    )
    products = dot_tn(normed_ref[...].reshape(count * tok_count, width), grads)
    small = [0.0] * 4
    for at in range(count):
        for rows in tiles(tok_count):
            places = slice(at * tok_count + rows.start, at * tok_count + rows.stop)
            normed, scale = normalize(tokens_ref[at, rows].astype(F32))
            given = grad_normed[places]
            sums = [
                grads_ref[at, rows, :width].astype(F32),
                grads_ref[at, rows, 2 * width :].astype(F32),
                given * normed,
                given,
            ]
            small = [total + partial_sum(part) for total, part in zip(small, sums)]
            back = normalize_back(given * gain, normed, scale)
            input_grad_ref[at, rows] = grad_middle_ref[at, rows] + back
    for at, total in enumerate(small):
        small_ref[2:3, at * width : (at + 1) * width] += column_sum(total)
    for rows in tiles(width):
        weights_ref[rows, : 3 * width] += products[rows]

    @pl.when(sequence == pl.num_programs(0) - 1)
    def _():
        parts = small_ref.shape[1] // CHUNK
        for line in range(3):
            for part in range(parts):
                at = line * parts + part
                weights_ref[at : at + 1, 3 * width :] = small_ref[
                    line : line + 1, part * CHUNK : (part + 1) * CHUNK
                ]
        split_rows(weights_ref, shard_ref[1], send_ref.at[0], keep_ref.at[0])


def half_of(ref, bit):
    rows = ref.shape[1] // 2
    return ref[:, pl.ds(pl.multiple_of(bit * rows, 8), rows), :]


def first_sum_kernel(fetch, bits_ref, keep_ref, other_ref, token_ref, send_ref, next_ref, *scratch):
    rows = send_ref.shape[1]
    begin = pl.multiple_of((1 - bits_ref[1]) * rows, 8)
    fetched_ref, sems = scratch
    copies = []
    for at, ref in enumerate([keep_ref, other_ref][:fetch]):
        source = ref.at[:, pl.ds(begin, rows), :]
        copies.append(pltpu.make_async_copy(source, fetched_ref.at[at], sems.at[at]))
        copies[-1].start()
    for copy in copies:
        copy.wait()
    other = fetched_ref[1] if fetch > 1 else other_ref[:, pl.ds(begin, rows), :]
    send_ref[...] = fetched_ref[0] + other


def second_sum_kernel(
    fetch, bits_ref, keep_ref, other_ref, new_ref, token_ref, send_ref, stay_ref, next_ref, *scratch
):
    rows = new_ref.shape[1]
    half = rows // 2
    begin = pl.multiple_of(bits_ref[1] * rows, 8)
    fetched_ref, sems = scratch
    copies = []
    for at, ref in enumerate([keep_ref, other_ref][:fetch]):
        source = ref.at[:, pl.ds(begin, rows), :]
        copies.append(pltpu.make_async_copy(source, fetched_ref.at[at], sems.at[at]))
        copies[-1].start()
    for copy in copies:
        copy.wait()
    for out_ref, bit in ((send_ref, 1 - bits_ref[2]), (stay_ref, bits_ref[2])):
        offset = pl.multiple_of(bit * half, 8)
        part = pl.ds(offset, half)
        if fetch > 1:
            other = fetched_ref[1, :, part, :]
        else:
            other = other_ref[:, pl.ds(pl.multiple_of(begin + offset, 8), half), :]
        out_ref[...] = fetched_ref[0, :, part, :] + other + new_ref[:, part, :]


def split_sum_kernel(
    step, bits_ref, keep_ref, new_ref, token_ref, send_ref, stay_ref, next_ref
):
    bit = bits_ref[step]
    send_ref[...] = half_of(keep_ref, 1 - bit) + half_of(new_ref, 1 - bit)
    stay_ref[...] = half_of(keep_ref, bit) + half_of(new_ref, bit)


def last_sum_kernel(bits_ref, keep_ref, new_ref, token_ref, out_ref, next_ref):
    out_ref[...] = keep_ref[...] + new_ref[...]


def join_rows_kernel(step, bits_ref, own_ref, other_ref, token_ref, out_ref, next_ref):
    rows = own_ref.shape[1]
    bit = bits_ref[step]
    out_ref[:, pl.ds(pl.multiple_of(bit * rows, 8), rows), :] = own_ref[...]
    out_ref[:, pl.ds(pl.multiple_of((1 - bit) * rows, 8), rows), :] = other_ref[...]


def place_down_kernel(bits_ref, own_ref, other_ref, token_ref, out_ref, next_ref):
    rows = own_ref.shape[1]
    core = bits_ref[0]
    out_ref[pl.ds(pl.multiple_of(core * rows, 8), rows), :] = own_ref[0]
    out_ref[pl.ds(pl.multiple_of((1 - core) * rows, 8), rows), :] = other_ref[0]


def place_up_kernel(bits_ref, own_ref, other_ref, token_ref, up_ref, output_ref, next_ref):
    parts, rows, width = own_ref.shape
    core = bits_ref[0]
    for side in range(2):

        @pl.when(core == side)
        def _():
            for half, source in ((side, own_ref), (1 - side, other_ref)):
                for part in range(parts - 1):
                    column = (half * (parts - 1) // 2 + part // 2) * width
                    row = part % 2 * rows
                    up_ref[row : row + rows, column : column + width] = source[part]
                output_ref[half * rows : (half + 1) * rows, :] = source[parts - 1]


def place_last_kernel(vectors, bits_ref, own_ref, other_ref, token_ref, *refs):
    rows = own_ref.shape[1]
    core = bits_ref[0]
    outs, extra_ref = refs[:3], refs[-1]
    for half, source in ((core, own_ref), (1 - core, other_ref)):
        begin = pl.multiple_of(half * rows, 8)
        width = outs[0].shape[1]
        for at, out in enumerate(outs):
            out[pl.ds(begin, rows), :] = source[0, :, at * width : (at + 1) * width]
        extra_ref[pl.ds(begin, rows), :] = source[0, :, 3 * width :]
    row = 0
    for out in refs[3:-2]:
        for part in range(out.shape[1] // CHUNK):
            out[:, part * CHUNK : (part + 1) * CHUNK] = extra_ref[row : row + 1, :]
            row += 1


class Reducer:
    def __init__(self):
        self.shards = lax.axis_size("seq")
        self.batches = lax.axis_size("batch")
        seq_bits = self.shards.bit_length() - 1
        far_bits = self.batches.bit_length() - 2
        seq_half, far_half = seq_bits // 2, far_bits // 2
        orders = (
            [("seq", bit) for bit in range(seq_bits)]
            + [("batch", bit + 1) for bit in range(far_bits)],
            [("seq", (bit + seq_half) % seq_bits) for bit in range(seq_bits)]
            + [("batch", (bit + far_half) % far_bits + 1) for bit in range(far_bits)],
        )
        places = dict(seq=lax.axis_index("seq"), batch=lax.axis_index("batch"))
        core = places["batch"] & 1
        bits = [core]
        for first, second in zip(*orders):
            one, other = [(places[axis] >> bit) & 1 for axis, bit in (first, second)]
            bits.append(jnp.where(core == 0, one, other))
        self.steps = len(bits)
        self.token = None
        self.bits = jnp.stack(bits).astype(jnp.int32)
        self.pairs = [[] for _ in bits]
        for seq in range(self.shards):
            for batch in range(self.batches):
                moves = [("batch", 0)] + orders[batch & 1]
                for pairs, (axis, bit) in zip(self.pairs, moves):
                    to_seq = seq ^ (1 << bit) if axis == "seq" else seq
                    to_batch = batch ^ (1 << bit) if axis == "batch" else batch
                    pairs.append((seq * self.batches + batch, to_seq * self.batches + to_batch))

    def swap(self, array, step):
        return lax.ppermute(array, ("seq", "batch"), self.pairs[step])

    def run(self, kernel, name, in_specs, operands, out_specs, shapes, scratch=(), chunk=None, limit=32 * 2**20):
        anywhere = pl.BlockSpec(memory_space=pl.ANY)
        *outs, self.token = pl.pallas_call(
            kernel,
            in_specs=[pl.BlockSpec(memory_space=pltpu.SMEM)] + in_specs + [anywhere],
            out_specs=out_specs + [anywhere],
            out_shape=[jax.ShapeDtypeStruct(shape, F32) for shape in shapes + [TOKEN]],
            scratch_shapes=scratch,
            compiler_params=pltpu.CompilerParams(vmem_limit_bytes=limit),
            cost_estimate=pl.CostEstimate(
                flops=0, bytes_accessed=ROUND_BYTES[chunk], transcendentals=0
            ),
            name=name,
        )(self.bits, *operands, self.token)
        return outs

    def gate(self, name, *arrays):
        anywhere = pl.BlockSpec(memory_space=pl.ANY)
        *arrays, self.token = pl.pallas_call(
            lambda *refs: None,
            in_specs=[anywhere] * (len(arrays) + 1),
            out_specs=[anywhere] * (len(arrays) + 1),
            out_shape=[
                jax.ShapeDtypeStruct(shape, F32)
                for shape in [array.shape for array in arrays] + [TOKEN]
            ],
            input_output_aliases={at: at for at in range(len(arrays))},
            cost_estimate=pl.CostEstimate(flops=0, bytes_accessed=0, transcendentals=0),
            name=f"{name}_gate",
        )(*arrays, self.token)
        return arrays

    def total(self, name, terms, step, fetch):
        parts, full, width = terms[0].shape
        anywhere, vmem = pl.BlockSpec(memory_space=pl.ANY), pl.BlockSpec(memory_space=pltpu.VMEM)
        given = [anywhere] * fetch + [vmem] * (2 - fetch)
        if step <= 2:
            scratch = [
                pltpu.VMEM((fetch, parts, full // 2, width), F32),
                pltpu.SemaphoreType.DMA((fetch,)),
            ]
        if step == 1:
            kernel = functools.partial(first_sum_kernel, fetch)
            shapes = [(parts, full // 2, width)]
            (send,) = self.run(
                kernel, f"{name}_sum1", given, terms, [vmem], shapes, scratch, chunk=name
            )
            return send, terms
        if step == 2:
            kernel = functools.partial(second_sum_kernel, fetch)
            shapes = [(parts, full // 4, width)] * 2
            send, stay = self.run(
                kernel,
                f"{name}_sum2",
                given + [vmem],
                terms,
                [vmem] * 2,
                shapes,
                scratch,
                chunk=name,
                limit=VMEM_BYTES if fetch > 1 else 32 * 2**20,
            )
            return send, [stay]
        kernel = functools.partial(split_sum_kernel, step)
        shapes = [(parts, full // 2, width)] * 2
        send, stay = self.run(
            kernel, f"{name}_sum{step}", [vmem] * 2, terms, [vmem] * 2, shapes, chunk=name
        )
        return send, [stay]

    def finish(self, name, terms):
        vmem = pl.BlockSpec(memory_space=pltpu.VMEM)
        (out,) = self.run(
            last_sum_kernel, f"{name}_total", [vmem] * 2, terms, [vmem], [terms[0].shape], chunk=name
        )
        return out

    def join(self, name, own, other, step):
        parts, rows, width = own.shape
        vmem = pl.BlockSpec(memory_space=pltpu.VMEM)
        (out,) = self.run(
            functools.partial(join_rows_kernel, step),
            f"{name}_join{step}",
            [vmem, vmem],
            [own, other],
            [vmem],
            [(parts, 2 * rows, width)],
            chunk=name,
        )
        return out

    def place(self, name, kernel, own, other, shapes, scratch=()):
        vmem = pl.BlockSpec(memory_space=pltpu.VMEM)
        return self.run(
            kernel,
            f"{name}_place",
            [vmem, vmem],
            [own, other],
            [vmem] * len(shapes),
            shapes,
            scratch,
            chunk=name,
        )


class Chunk:
    def __init__(
        self,
        reducer,
        name,
        send,
        keep,
        kernel,
        shapes,
        scratch=(),
        gated=False,
        fetch=2,
    ):
        self.reducer, self.name = reducer, name
        self.last = reducer.steps - 1
        self.fits = keep.shape[1] >> self.last >= 8
        self.send, self.terms, self.gated, self.fetch = send, [keep], gated, fetch
        self.kernel, self.shapes, self.scratch = kernel, list(shapes), scratch
        self.outs = self.ready = None
        self.stages = self.run()

    def run(self):
        reducer, name, last = self.reducer, self.name, self.last
        if not self.fits:
            outs = reducer.place(
                name, self.kernel, self.terms[0], self.send, self.shapes, self.scratch
            )
            self.outs = lax.psum(outs, ("seq", "batch"))
            return
        if self.gated:
            (self.send,) = reducer.gate(name, self.send)
        self.terms = terms = self.terms + [reducer.swap(self.send, 0)]
        for step in range(1, last + 1):
            yield
            if step == 1 and self.ready is not None:
                send = self.ready
                if name == "down":
                    (send,) = reducer.gate(name, send)
            else:
                send, terms = reducer.total(name, terms, step, self.fetch)
            terms = terms + [reducer.swap(send, step)]
        yield
        block = reducer.finish(name, terms)
        for step in range(last, 0, -1):
            other = reducer.swap(block, step)
            yield
            block = reducer.join(name, block, other, step)
        other = reducer.swap(block, 0)
        yield
        self.outs = reducer.place(name, self.kernel, block, other, self.shapes, self.scratch)

    def first_sum(self, cuts):
        if not self.fits:
            return [], [], [pl.BlockSpec(TOKEN, lambda at, *_: (0, 0))], [(TOKEN, F32)]
        parts, full, width = self.terms[0].shape
        rows = full // 2
        block = (parts, rows // cuts, width)
        given = pl.BlockSpec(block, lambda at, *scalars: (0, (1 - scalars[2][1]) * cuts + at, 0))
        made = pl.BlockSpec(block, lambda at, *_: (0, at, 0))
        return self.terms, [given] * 2, [made], [((parts, rows, width), F32)]

    def forward(self):
        return next(self.stages, self) is not self


def by_sequence(*shape, begin=0, count=1):
    return pl.BlockSpec((count,) + shape, lambda at, *_: (at + begin,) + (0,) * len(shape))


def whole(*shape):
    return pl.BlockSpec(shape, lambda at, *_: (0,) * len(shape))


def call(
    reducer,
    kernel,
    grid,
    in_specs,
    out_specs,
    out_shapes,
    flops,
    operands,
    aliases=None,
    scratch=(),
    prefetch=2,
):
    anywhere = pl.BlockSpec(memory_space=pl.ANY)
    given, made = len(in_specs), len(out_specs)
    tokens = [] if reducer.token is None else [reducer.token]

    def body(*refs):
        inputs = refs[: prefetch + given]
        rest = refs[prefetch + given + len(tokens) :]
        kernel(*inputs, *rest[:made], *rest[made + 1 :])

    *outs, reducer.token = pl.pallas_call(
        body,
        grid_spec=pltpu.PrefetchScalarGridSpec(
            num_scalar_prefetch=prefetch,
            grid=grid,
            in_specs=in_specs + [anywhere] * len(tokens),
            out_specs=out_specs + [anywhere],
            scratch_shapes=scratch,
        ),
        out_shape=[
            jax.ShapeDtypeStruct(shape, dtype) for shape, dtype in out_shapes + [(TOKEN, F32)]
        ],
        input_output_aliases=aliases or {},
        compiler_params=pltpu.CompilerParams(
            dimension_semantics=("arbitrary",), vmem_limit_bytes=VMEM_BYTES
        ),
        cost_estimate=pl.CostEstimate(flops=flops, bytes_accessed=20_000_000, transcendentals=0),
    )(*operands, *tokens)
    return outs


def local(
    tokens,
    lengths,
    query_weight,
    key_weight,
    value_weight,
    output_weight,
    up_weight,
    down_weight,
    query_bias,
    value_bias,
    output_bias,
    up_bias,
    down_bias,
    first_gain,
    first_shift,
    second_gain,
    second_shift,
    cotangent,
):
    seq_count, tok_count, width = tokens.shape
    inner_width = up_weight.shape[1]
    shards = lax.axis_size("seq")
    shard_index = lax.axis_index("seq")
    heights = shards.bit_length() - 1
    grid = (seq_count,)
    reducer = Reducer()
    core = reducer.bits[:1]
    shard = jnp.stack([shard_index.astype(jnp.int32), reducer.bits[0]])

    def row(vector):
        return vector.reshape(1, -1)

    groups = []
    for height in range(heights):
        members = group_members(tok_count, BLOCK << height)
        groups.append(np.pad(members, ((0, max(8 - members.shape[0], 0)), (0, 0))))
    groups = jnp.asarray(np.concatenate(groups, axis=0), BF16)
    members = jnp.asarray(coarse_members(tok_count), BF16)
    spots = jnp.asarray(coarse_members(tok_count).T, BF16)
    near_spread = jnp.asarray(np.concatenate([averaging(at) for at in range(1, 4)], axis=1), BF16)
    near_pair = jnp.asarray(np.stack([averaging_pair(at) for at in range(1, 4)]), BF16)
    far_pair = jnp.asarray(np.stack([averaging_pair(4 + at) for at in range(heights)]), BF16)

    fine = by_sequence(tok_count, width)
    tall = by_sequence(width, tok_count)
    heads = by_sequence(HEADS, tok_count)
    square = whole(width, width)
    vector = whole(1, width)
    fine_shape = (seq_count, tok_count, width)
    tall_shape = (seq_count, width, tok_count)
    heads_shape = (seq_count, HEADS, tok_count)
    sum_shapes = [(BLOCK >> height, 2 * width) for height in range(heights)]
    together = 2 - seq_count % 2
    some_fine = by_sequence(tok_count, width, count=together)
    some_tall = by_sequence(width, tok_count, count=together)
    queries, keys, values, *sums = call(
        reducer,
        functools.partial(project_kernel, heights),
        (seq_count // together,),
        [some_fine, square, square, square, vector, vector, vector, vector, whole(*groups.shape)],
        [some_tall, some_fine, some_fine]
        + [by_sequence(*shape, count=together) for shape in sum_shapes],
        [(tall_shape, BF16), (fine_shape, BF16), (fine_shape, BF16)]
        + [((seq_count,) + shape, F32) for shape in sum_shapes],
        2 * seq_count * tok_count * width * width * 3,
        scratch=[pltpu.VMEM((together, tok_count, width), BF16)] * 2,
        operands=[lengths,
        shard,
        tokens,
        query_weight,
        key_weight,
        value_weight,
        row(query_bias),
        row(value_bias),
        row(first_gain),
        row(first_shift),
        groups],
    )

    def swap(array, mask):
        return lax.ppermute(array, "seq", [(at, at ^ mask) for at in range(shards)])

    received = [swap(sums[mask.bit_length() - 1], mask) for mask in range(1, shards)]
    pieces = received[:3]
    for height in range(2, heights):
        pieces.append(
            jnp.concatenate(received[(1 << height) - 1 : (2 << height) - 1], axis=1)
        )
    piece_shapes = [piece.shape[1:] for piece in pieces]
    piece_specs = [by_sequence(*shape, count=together) for shape in piece_shapes]

    spread_shape = (seq_count, width, 2 * near_spread.shape[1])
    pool_shape = (seq_count, members.shape[0], width)
    spread_block, pool_block = by_sequence(*spread_shape[1:]), by_sequence(*pool_shape[1:])
    maxima, totals, numer, near_queries, pooled_near_keys, pooled_near_values = call(
        reducer,
        near_kernel,
        grid,
        [tall, fine, fine, whole(*members.shape), whole(*near_spread.shape)],
        [heads, heads, tall, spread_block, pool_block, pool_block],
        [
            (heads_shape, F32),
            (heads_shape, F32),
            (tall_shape, BF16),
            (spread_shape, BF16),
            (pool_shape, BF16),
            (pool_shape, BF16),
        ],
        1_000_000_000,
        [lengths, shard, queries, keys, values, members, near_spread],
    )

    some_heads = by_sequence(HEADS, tok_count, count=together)
    middle, second, outs, level, all_far_queries = call(
        reducer,
        functools.partial(join_kernel, heights, shards, len(pieces)),
        (seq_count // together,),
        [
            some_fine,
            some_tall,
            some_heads,
            some_heads,
            some_tall,
            square,
            vector,
            vector,
            vector,
            whole(*far_pair.shape),
        ]
        + [pl.BlockSpec(memory_space=pltpu.VMEM)] * len(pieces),
        [some_fine, some_fine, some_tall, some_heads]
        + [by_sequence(width, heights * tok_count, count=together)],
        [
            (fine_shape, F32),
            (fine_shape, BF16),
            (tall_shape, F32),
            (heads_shape, F32),
            ((seq_count, width, heights * tok_count), BF16),
        ],
        2 * seq_count * tok_count * width * width,
        scratch=[pltpu.VMEM((together, width, tok_count), BF16)],
        operands=[lengths,
        shard,
        tokens,
        queries,
        maxima,
        totals,
        numer,
        output_weight,
        row(output_bias),
        row(second_gain),
        row(second_shift),
        far_pair,
        *pieces],
    )

    steps = inner_width // width
    half_steps = steps // 2
    all_rows = whole(*fine_shape)

    def turned(at, core):
        return lax.rem(at + half_steps * (1 - core[0]), steps)

    columns = pl.BlockSpec((width, width), lambda at, core: (0, turned(at, core)))
    column_row = pl.BlockSpec((1, width), lambda at, core: (0, turned(at, core)))
    blocks = pl.BlockSpec((width, width), lambda at, core: (turned(at, core), 0))
    rows_count = seq_count * tok_count
    half_width = width // 2
    parts = steps + 1

    def halves(block, axis):
        def place(at):
            return tuple(at if place == axis else 0 for place in range(3))

        return [
            pl.BlockSpec(block, lambda at, core: place(jnp.minimum(at, half_steps - 1))),
            pl.BlockSpec(block, lambda at, core: place(jnp.maximum(at - half_steps, 0))),
        ]

    grad_second, down_send, down_keep, up_send, up_keep, grad_up_bias, hidden = call(
        reducer,
        functools.partial(hidden_kernel, steps),
        (steps,),
        [all_rows, all_rows, columns, blocks, column_row],
        [all_rows]
        + halves((1, width, width), 1)
        + halves((2, half_width, width), 0)
        + [column_row, pl.BlockSpec((rows_count, width), lambda at, core: (0, turned(at, core)))],
        [
            (fine_shape, BF16),
            ((1, inner_width // 2, width), F32),
            ((1, inner_width // 2, width), F32),
            ((parts, half_width, width), F32),
            ((parts, half_width, width), F32),
            ((1, inner_width), F32),
            ((rows_count, inner_width), BF16),
        ],
        2 * rows_count * width * 5 * inner_width,
        [core, second, cotangent, up_weight, down_weight, row(up_bias)],
        scratch=[
            pltpu.VMEM(fine_shape, F32),
            pltpu.VMEM((width, rows_count), BF16),
            pltpu.VMEM((rows_count, width), BF16),
        ],
        prefetch=1,
    )
    chunk_down = Chunk(
        reducer,
        "down",
        down_send,
        down_keep,
        place_down_kernel,
        [(inner_width, width)],
    )
    chunk_down.forward()

    grad_middle, grad_attended, inner_sums, far_queries, *rest = call(
        reducer,
        functools.partial(backward_kernel, heights, shards, len(pieces)),
        (seq_count // together,),
        [
            some_fine,
            by_sequence(width, heights * tok_count, count=together),
            some_fine,
            some_tall,
            some_heads,
            some_fine,
            square,
            vector,
            whole(*far_pair.shape),
        ]
        + [pl.BlockSpec(memory_space=pltpu.VMEM)] * len(pieces)
        + [pl.BlockSpec(memory_space=pl.ANY)] * 2,
        [some_fine, some_tall, some_heads, some_tall]
        + piece_specs
        + [pl.BlockSpec((1, half_width, width), lambda at, *_: (parts - 1, 0, 0))] * 2
        + [whole(1, inner_width)],
        [
            (fine_shape, F32),
            (tall_shape, BF16),
            (heads_shape, F32),
            (tall_shape, BF16),
        ]
        + [((seq_count,) + shape, F32) for shape in piece_shapes]
        + [((parts, half_width, width), F32)] * 2
        + [((1, inner_width), F32)],
        2 * rows_count * width * 2 * width,
        [lengths,
        shard,
        cotangent,
        all_far_queries,
        middle,
        outs,
        level,
        grad_second,
        output_weight,
        row(second_gain),
        far_pair,
        *pieces,
        up_send,
        up_keep],
        aliases={
            11 + len(pieces): 4 + len(pieces),
            12 + len(pieces): 5 + len(pieces),
        },
        scratch=[
            pltpu.VMEM((width, width), F32),
            pltpu.VMEM((together, tok_count, width), BF16),
            pltpu.VMEM((together, width, tok_count), BF16),
        ],
    )
    grad_pieces = rest[: len(pieces)]
    up_send, up_keep, small_middle = rest[len(pieces) :]
    chunk_up = Chunk(
        reducer,
        "up",
        up_send,
        up_keep,
        place_up_kernel,
        [(width, inner_width), (width, width)],
    )
    turns, layer = dict(d=chunk_down, u=chunk_up), []

    def take(place):
        for turn in ROUNDS.split(",")[place]:
            if turn == "o":
                layer.extend(
                    call(
                        reducer,
                        output_kernel,
                        grid,
                        [
                            pl.BlockSpec((tok_count, inner_width), lambda at, *_: (at, 0)),
                            fine,
                            whole(inner_width, width),
                            vector,
                        ],
                        [fine],
                        [(fine_shape, BF16)],
                        2 * rows_count * width * inner_width,
                        [core, hidden, middle, down_weight, row(down_bias)],
                        prefetch=1,
                    )
                )
            else:
                turns[turn].forward()

    returned = []
    for mask in range(1, shards):
        height = mask.bit_length() - 1
        if height < 2:
            piece = grad_pieces[mask - 1]
        else:
            rows = BLOCK >> height
            begin = (mask - (1 << height)) * rows
            piece = grad_pieces[height + 1][:, begin : begin + rows]
        returned.append(swap(piece, mask))
    take(0)
    half = seq_count // 2
    near_grads = ()
    anywhere = pl.BlockSpec(memory_space=pl.ANY)
    for begin in (0, half):
        some = functools.partial(by_sequence, begin=begin)
        some_fine, some_tall = some(tok_count, width), some(width, tok_count)
        some_heads = some(HEADS, tok_count)
        in_specs = [
            some_tall,
            some_fine,
            some_fine,
            some_tall,
            some_heads,
            some_heads,
            whole(*spots.shape),
            whole(*near_pair.shape),
            some_tall,
            some(*spread_shape[1:]),
            some(*pool_shape[1:]),
            some(*pool_shape[1:]),
        ]
        chunk = chunk_up if begin else chunk_down
        terms, sum_in, sum_out, sum_shape = chunk.first_sum(half)
        *near_grads, send = call(
            reducer,
            functools.partial(near_back_kernel, begin, len(terms) > 0),
            (half,),
            in_specs + [anywhere] * len(near_grads) + sum_in,
            [some_tall, some_fine, some_fine] + sum_out,
            [(tall_shape, BF16), (fine_shape, F32), (fine_shape, BF16)] + sum_shape,
            2_000_000_000,
            [
                lengths,
                shard,
                reducer.bits,
                queries,
                keys,
                values,
                grad_attended,
                level,
                inner_sums,
                spots,
                near_pair,
                far_queries,
                near_queries,
                pooled_near_keys,
                pooled_near_values,
                *near_grads,
                *terms,
            ],
            {3 + len(in_specs) + at: at for at in range(len(near_grads))},
            prefetch=3,
        )
        chunk.ready = send
        if begin == 0:
            returned = reducer.gate("far", *returned)
            take(1)
    take(2)

    back_pieces, back_heights = [], []
    for mask in range(1, shards):
        height = mask.bit_length() - 1
        if height < 2:
            back_pieces.append(returned[mask - 1])
            back_heights.append(height)
    for height in range(2, heights):
        total = sum(returned[(1 << height) - 1 : (2 << height) - 1])
        back_pieces.append(jnp.pad(total, ((0, 0), (0, 8 - total.shape[1]), (0, 0))))
        back_heights.append(height)
    some_fine = by_sequence(tok_count, width, count=together)
    some_tall = by_sequence(width, tok_count, count=together)
    input_grad, last_send, last_keep = call(
        reducer,
        functools.partial(last_kernel, heights, tuple(back_heights)),
        (seq_count // together,),
        [
            some_fine,
            some_fine,
            some_tall,
            some_fine,
            some_fine,
            square,
            square,
            square,
            vector,
            vector,
            whole(*groups.shape),
            whole(1, inner_width),
            whole(1, inner_width),
        ]
        + [by_sequence(*piece.shape[1:], count=together) for piece in back_pieces],
        [some_fine] + [whole(1, half_width, 3 * width + CHUNK)] * 2,
        [(fine_shape, F32)] + [((1, half_width, 3 * width + CHUNK), F32)] * 2,
        2 * seq_count * tok_count * width * width * 6,
        [lengths,
        shard,
        tokens,
        grad_middle,
        *near_grads,
        query_weight,
        key_weight,
        value_weight,
        row(first_gain),
        row(first_shift),
        groups,
        grad_up_bias,
        small_middle,
        *back_pieces],
        scratch=[
            pltpu.VMEM((width, 3 * width + CHUNK), F32),
            pltpu.VMEM((8, inner_width), F32),
            pltpu.VMEM((together, tok_count, width), BF16),
            pltpu.VMEM((together, tok_count, 3 * width), BF16),
        ],
    )
    vectors = [inner_width] + [width] * 8
    chunk_last = Chunk(
        reducer,
        "last",
        last_send,
        last_keep,
        functools.partial(place_last_kernel, vectors),
        [(width, width)] * 3 + [(1, length) for length in vectors],
        [pltpu.VMEM((width, CHUNK), F32)],
        gated=True,
        fetch=1,
    )
    turns["l"] = chunk_last
    take(3)
    for chunk in turns.values():
        while chunk.forward():
            pass
    grad_query, grad_key, grad_value, *vectors = chunk_last.outs
    (grad_down,) = chunk_down.outs
    grad_up, grad_output = chunk_up.outs
    (
        grad_up_bias,
        grad_down_bias,
        grad_second_gain,
        grad_second_shift,
        grad_output_bias,
        grad_query_bias,
        grad_value_bias,
        grad_first_gain,
        grad_first_shift,
    ) = [vector.reshape(-1) for vector in vectors]
    return (
        layer[0],
        input_grad,
        grad_query,
        grad_key,
        grad_value,
        grad_output,
        grad_up,
        grad_down,
        grad_query_bias,
        grad_value_bias,
        grad_output_bias,
        grad_up_bias,
        grad_down_bias,
        grad_first_gain,
        grad_first_shift,
        grad_second_gain,
        grad_second_shift,
    )


def solution(mesh):
    rows = P("batch", "seq", None)
    return jax.shard_map(
        local,
        mesh=mesh,
        in_specs=(rows, P("batch")) + (P(),) * 15 + (rows,),
        out_specs=(rows, rows) + (P(),) * 15,
        check_vma=False,
    )
```

```python
import functools

import jax
import jax.numpy as jnp
import numpy as np
from jax import lax
from jax.experimental import pallas as pl
from jax.experimental.pallas import tpu as pltpu
from jax.sharding import PartitionSpec as P

HEADS = 8
BLOCK = 16
CHUNK = 128
PAIR = 128
HALF = 64
LOCAL_ROWS = (128, 64, 32, 16)
LOCAL_STARTS = (0, 128, 192, 224)
LOCAL_KEYS = 240
COARSE_KEYS = 112
MASKED = -1e30
TOKEN = (8, 128)
ROUND_BYTES = dict(down=40_000_000, up=40_000_000, last=40_000_000)
ROUNDS = "u,d,ud,dudldluudlluddlululudlouldlul"
TILE = 32
EPSILON = 1e-05
VMEM_BYTES = 62 * 2**20
F32 = jnp.float32
BF16 = jnp.bfloat16


def dot(left, right):
    return lax.dot_general(left, right, (((1,), (0,)), ((), ())), preferred_element_type=F32)


def dot_nt(left, right):
    return lax.dot_general(left, right, (((1,), (1,)), ((), ())), preferred_element_type=F32)


def dot_tn(left, right):
    return lax.dot_general(left, right, (((0,), (0,)), ((), ())), preferred_element_type=F32)


def iota(shape, axis):
    return lax.broadcasted_iota(jnp.int32, shape, axis)


def row_mean(values):
    return jnp.mean(values, axis=-1, keepdims=True)


def column_sum(values):
    return jnp.sum(values, axis=0, keepdims=True)


def normalize(values):
    center = values - row_mean(values)
    scale = lax.rsqrt(row_mean(center * center) + EPSILON)
    return center * scale, scale


def normalize_back(grads, normed, scale):
    return scale * (grads - row_mean(grads) - normed * row_mean(grads * normed))


def block_diagonal(block):
    zeros = jnp.zeros((HALF, CHUNK), block.dtype)
    first = jnp.concatenate([block[:HALF], zeros], axis=1)
    second = jnp.concatenate([zeros, block[HALF:]], axis=1)
    return jnp.concatenate([first, second], axis=0)


def diagonal_blocks(wide):
    return jnp.concatenate([wide[:HALF, :CHUNK], wide[HALF:, CHUNK:]], axis=0)


def head_rows(row):
    first = jnp.broadcast_to(row[:, :CHUNK], (HALF, CHUNK))
    second = jnp.broadcast_to(row[:, CHUNK:], (HALF, CHUNK))
    return jnp.concatenate([first, second], axis=0)


def twice(block):
    return jnp.concatenate([block, block], axis=1)


def four_times(block):
    return jnp.concatenate([block, block, block, block], axis=1)


def averaging(level):
    spots = np.arange(CHUNK) >> level
    return (spots[:, None] == spots[None, :]).astype(np.float32) / (1 << level)


def averaging_pair(level):
    return np.kron(np.eye(2, dtype=np.float32), averaging(level))


def coarse_members(tok_count):
    spots = np.arange(tok_count)
    rows = []
    for chunk in range(2):
        for level in range(1, 4):
            first = (chunk if level < 3 else 1 - chunk) * CHUNK
            begins = first + (np.arange(LOCAL_ROWS[level]) << level)
            inside = spots[None, :] - begins[:, None]
            rows.append((inside >= 0) & (inside < (1 << level)))
    return np.concatenate(rows, axis=0).astype(np.float32)


def group_members(tok_count, factor):
    spots = np.arange(tok_count) // factor
    return (np.arange(tok_count // factor)[:, None] == spots[None, :]).astype(np.float32)


def local_counts(remaining, chunk, level):
    rows = LOCAL_ROWS[level]
    spots = iota((rows, CHUNK), 0) << level
    first = (chunk if level < 3 else 1 - chunk) * CHUNK
    return jnp.clip(remaining - (first + spots), 0, 1 << level), spots


def local_bias(remaining, chunk):
    parts = []
    for level in range(4):
        counts, spots = local_counts(remaining, chunk, level)
        allowed = counts > 0
        places = iota(counts.shape, 1)
        if level == 0:
            allowed = allowed & ((spots >> 5) == (places >> 5))
        elif level < 3:
            allowed = allowed & (((spots >> (4 + level)) ^ (places >> (4 + level))) == 1)
        logs = jnp.log(jnp.maximum(counts, 1).astype(F32))
        parts.append(jnp.where(allowed, logs, MASKED))
    return parts


def coarse_inverse(remaining):
    parts = []
    for chunk in range(2):
        for level in range(1, 4):
            counts, _ = local_counts(remaining, chunk, level)
            parts.append(1.0 / jnp.maximum(counts, 1).astype(F32))
    return jnp.concatenate(parts, axis=0)


def pooled_keys(members, rows, inverse):
    return (dot(members, rows) * four_times(inverse)).astype(BF16)


def chunk_keys(rows, pooled):
    return [
        jnp.concatenate(
            [
                rows[chunk * CHUNK : (chunk + 1) * CHUNK],
                pooled[chunk * COARSE_KEYS : (chunk + 1) * COARSE_KEYS],
            ],
            axis=0,
        )
        for chunk in range(2)
    ]


def level_queries(queries, coarse, chunk):
    levels = coarse.shape[1] // CHUNK // 2
    parts = [queries[:, chunk * CHUNK : (chunk + 1) * CHUNK]]
    for at in range(chunk * levels, (chunk + 1) * levels):
        parts.append(coarse[:, at * CHUNK : (at + 1) * CHUNK])
    return parts


UNITS = [(chunk, pair) for chunk in range(2) for pair in range(HEADS // 2)]


def skewed(first, *stages):
    held = {}
    for tick in range(len(UNITS) + len(stages)):
        for stage in range(len(stages) + 1):
            at = tick - stage
            if 0 <= at < len(UNITS):
                unit = UNITS[at]
                if stage == 0:
                    held[unit] = first(unit)
                else:
                    held[unit] = stages[stage - 1](unit, held[unit])
    return held


def interleaved(work, count):
    runs = [work(at) for at in range(count)]
    while runs:
        runs = [run for run in runs if next(run, run) is not run]


def pair_of(index):
    return slice(index * PAIR, (index + 1) * PAIR)


def local_logits(keys, tall, pair):
    return [
        dot(
            keys[LOCAL_STARTS[level] : LOCAL_STARTS[level] + LOCAL_ROWS[level], pair_of(pair)],
            tall[level],
        )
        for level in range(4)
    ]


def tiles(rows, size=TILE):
    return [slice(begin, begin + size) for begin in range(0, rows, size)]


def partial_sum(values):
    return jnp.sum(values.reshape(-1, 8, values.shape[1]), axis=0)


def add_to(ref, values):
    for rows in tiles(values.shape[0]):
        ref[rows, :] += values[rows]


def project_kernel(
    heights,
    lengths_ref,
    shard_ref,
    tokens_ref,
    query_weight_ref,
    key_weight_ref,
    value_weight_ref,
    query_bias_ref,
    value_bias_ref,
    gain_ref,
    shift_ref,
    groups_ref,
    queries_ref,
    keys_ref,
    values_ref,
    *refs,
):
    sums_refs, normed_ref, turned_ref = refs[:heights], refs[heights], refs[heights + 1]
    count, tok_count, width = tokens_ref.shape
    gain, shift = gain_ref[...], shift_ref[...]
    for at in range(count):
        for rows in tiles(tok_count):
            normed, _ = normalize(tokens_ref[at, rows].astype(F32))
            normed_ref[at, rows] = (normed * gain + shift).astype(BF16)
    normed = normed_ref[...].reshape(count * tok_count, width)
    keys_wide = dot(normed, key_weight_ref[...])
    values_wide = dot(normed, value_weight_ref[...])
    queries_wide = dot(normed, query_weight_ref[...])
    value_bias, query_bias = value_bias_ref[...], query_bias_ref[...]
    for at in range(count):
        remaining = lengths_ref[pl.program_id(0) * count + at] - shard_ref[shard_ref.shape[0] - 1] * tok_count
        for rows in tiles(tok_count):
            places = slice(at * tok_count + rows.start, at * tok_count + rows.stop)
            valid = iota((TILE, width), 0) + rows.start < remaining
            keys_ref[at, rows] = jnp.where(valid, keys_wide[places], 0.0).astype(BF16)
            values = values_wide[places] + value_bias
            values_ref[at, rows] = jnp.where(valid, values, 0.0).astype(BF16)
            turned_ref[at, rows] = ((queries_wide[places] + query_bias) * 0.125).astype(BF16)
        key_sums = dot(groups_ref[...], keys_ref[at])
        value_sums = dot(groups_ref[...], values_ref[at])
        begin = 0
        for height in range(heights):
            size = BLOCK >> height
            sums_refs[height][at, :, :width] = key_sums[begin : begin + size]
            sums_refs[height][at, :, width:] = value_sums[begin : begin + size]
            begin += max(size, 8)
        queries_ref[at] = turned_ref[at].T


def near_kernel(
    lengths_ref,
    shard_ref,
    queries_ref,
    keys_ref,
    values_ref,
    members_ref,
    spread_ref,
    maxima_ref,
    totals_ref,
    numer_ref,
    coarse_ref,
    pooled_keys_ref,
    pooled_values_ref,
):
    sequence = pl.program_id(0)
    tok_count = keys_ref.shape[1]
    remaining = lengths_ref[sequence] - shard_ref[shard_ref.shape[0] - 1] * tok_count
    inverse = coarse_inverse(remaining)
    pooled_keys_ref[0] = pooled_keys(members_ref[...], keys_ref[0], inverse)
    pooled_values_ref[0] = pooled_keys(members_ref[...], values_ref[0], inverse)
    keys = chunk_keys(keys_ref[0], pooled_keys_ref[0])
    values = chunk_keys(values_ref[0], pooled_values_ref[0])
    queries = queries_ref[0]
    bias = [local_bias(remaining, chunk) for chunk in range(2)]
    columns = spread_ref.shape[1]
    for chunk in range(2):
        own = queries[:, chunk * CHUNK : (chunk + 1) * CHUNK]
        coarse_ref[0, :, chunk * columns : (chunk + 1) * columns] = dot(
            own, spread_ref[...]
        ).astype(BF16)
    coarse = coarse_ref[0]
    levels = [level_queries(queries, coarse, chunk) for chunk in range(2)]

    def logits_of(unit):
        chunk, pair = unit
        tall = [block_diagonal(part[pair_of(pair)]) for part in levels[chunk]]
        return local_logits(keys[chunk], tall, pair)

    def softmax_of(unit, logits):
        chunk, pair = unit
        lanes = slice(chunk * CHUNK, (chunk + 1) * CHUNK)
        both = []
        for side in range(2):
            half = slice(side * CHUNK, (side + 1) * CHUNK)
            head = 2 * pair + side
            parts = [part[:, half] + extra for part, extra in zip(logits, bias[chunk])]
            maxima = functools.reduce(
                jnp.maximum, [jnp.max(part, axis=0, keepdims=True) for part in parts]
            )
            parts = [jnp.exp(part - maxima) for part in parts]
            maxima_ref[0, head : head + 1, lanes] = maxima
            totals = sum(partial_sum(part) for part in parts)
            totals_ref[0, head : head + 1, lanes] = column_sum(totals)
            both.append(jnp.concatenate([part.astype(BF16) for part in parts], axis=0))
        return jnp.concatenate(both, axis=1)

    def numer_of(unit, powers):
        chunk, pair = unit
        lanes = slice(chunk * CHUNK, (chunk + 1) * CHUNK)
        wide = dot_tn(values[chunk][:, pair_of(pair)], powers)
        numer_ref[0, pair_of(pair), lanes] = diagonal_blocks(wide).astype(BF16)

    skewed(logits_of, softmax_of, numer_of)


def split_rows(source_ref, core, send_ref, keep_ref):
    rows = send_ref.shape[0]
    send_ref[...] = source_ref[pl.ds(pl.multiple_of((1 - core) * rows, 8), rows), :]
    keep_ref[...] = source_ref[pl.ds(pl.multiple_of(core * rows, 8), rows), :]


def far_counts(length, shard, tok_count, heights, shards):
    spots = iota((BLOCK * heights, CHUNK), 0)
    begins = jnp.zeros_like(spots)
    widths = jnp.ones_like(spots)
    row = 0
    for mask in range(1, shards):
        height = mask.bit_length() - 1
        rows = BLOCK >> height
        inside = (spots >= row) & (spots < row + rows)
        first = jnp.bitwise_xor(shard, mask) * tok_count
        begins = jnp.where(inside, first + ((spots - row) << (4 + height)), begins)
        widths = jnp.where(inside, BLOCK << height, widths)
        row += rows
    return jnp.minimum(jnp.maximum(length - begins, 0), widths)


def half_lanes(shape, side):
    return iota(shape, 1) // HALF == side


def by_head(rows):
    blocks = []
    for head in range(HEADS):
        parts = [jnp.zeros((BLOCK, PAIR), F32)] * (HEADS // 2)
        part = rows[:, pair_of(head // 2)]
        parts[head // 2] = jnp.where(half_lanes(part.shape, head % 2), part, 0.0)
        blocks.append(jnp.concatenate(parts, axis=1))
    return jnp.concatenate(blocks, axis=0).astype(BF16)


def of_heads(wide):
    parts = []
    for pair in range(HEADS // 2):
        first = wide[2 * pair * BLOCK : (2 * pair + 1) * BLOCK, pair_of(pair)]
        second = wide[(2 * pair + 1) * BLOCK : (2 * pair + 2) * BLOCK, pair_of(pair)]
        parts.append(jnp.where(half_lanes(first.shape, 0), first, second))
    return jnp.concatenate(parts, axis=1)


def far_state(sequence, lengths_ref, shard, tok_count, heights, shards, pieces):
    counts = far_counts(lengths_ref[sequence], shard, tok_count, heights, shards)
    floored = jnp.maximum(counts, 1).astype(F32)
    inverse = four_times(1.0 / floored)
    bias = twice(jnp.where(counts > 0, jnp.log(floored), MASKED))
    bias = [bias[BLOCK * at : BLOCK * (at + 1)] for at in range(heights)]
    sums = jnp.concatenate([piece[sequence] for piece in pieces], axis=0)
    width = sums.shape[1] // 2
    keys, values = [], []
    for at in range(heights):
        rows = slice(BLOCK * at, BLOCK * (at + 1))
        keys.append(by_head(sums[rows, :width] * inverse[rows]))
        values.append(by_head(sums[rows, width:] * inverse[rows]))
    return keys, jnp.concatenate(values, axis=0), bias, inverse


def far_queries_of(queries, spread_ref, heights):
    return [dot(queries, spread_ref[at]).astype(BF16) for at in range(heights)]


def join_kernel(
    heights,
    shards,
    piece_count,
    lengths_ref,
    shard_ref,
    tokens_ref,
    queries_ref,
    maxima_ref,
    totals_ref,
    numer_ref,
    output_weight_ref,
    output_bias_ref,
    gain_ref,
    shift_ref,
    spread_ref,
    *refs,
):
    pieces = refs[:piece_count]
    middle_ref, second_ref, outs_ref, level_ref, far_ref, attended_ref = refs[piece_count:]
    count, tok_count, _ = tokens_ref.shape
    bias, gain, shift = output_bias_ref[...], gain_ref[...], shift_ref[...]

    def work(own):
        far_keys, far_values, far_bias, _ = far_state(
            pl.program_id(0) * count + own, lengths_ref, shard_ref[shard_ref.shape[0] - 1], tok_count, heights, shards, pieces
        )
        coarse = far_queries_of(queries_ref[own], spread_ref, heights)
        for at in range(heights):
            far_ref[own, :, at * tok_count : (at + 1) * tok_count] = coarse[at]
        logits = [dot(far_keys[at], coarse[at]) for at in range(heights)]
        yield
        powers = [[] for _ in range(heights)]
        fades, inverses = [], []
        for head in range(HEADS):
            rows = slice(BLOCK * head, BLOCK * (head + 1))
            near_maxima = maxima_ref[own, head : head + 1, :]
            parts = [logits[at][rows] + far_bias[at] for at in range(heights)]
            maxima = functools.reduce(jnp.maximum, parts)
            maxima = jnp.maximum(near_maxima, jnp.max(maxima, axis=0, keepdims=True))
            fade = jnp.exp(near_maxima - maxima)
            parts = [jnp.exp(part - maxima) for part in parts]
            totals = fade * totals_ref[own, head : head + 1, :] + column_sum(sum(parts))
            for at in range(heights):
                powers[at].append(parts[at].astype(BF16))
            level_ref[own, head : head + 1, :] = maxima + jnp.log(totals)
            inverse = 1.0 / totals
            fades.append(fade * inverse)
            inverses.append(inverse)
        yield
        far_numer = dot_tn(far_values, jnp.concatenate(sum(powers, []), axis=0))
        yield
        for head in range(HEADS):
            rows = slice(HALF * head, HALF * (head + 1))
            outs = numer_ref[own, rows, :].astype(F32) * fades[head] + far_numer[rows] * inverses[head]
            outs_ref[own, rows, :] = outs
            attended_ref[own, rows, :] = outs.astype(BF16)
        yield
        projected = dot_tn(attended_ref[own], output_weight_ref[...])
        yield
        for rows in tiles(tok_count):
            middle = tokens_ref[own, rows].astype(F32) + projected[rows] + bias
            middle_ref[own, rows] = middle
            normed, _ = normalize(middle)
            second_ref[own, rows] = (normed * gain + shift).astype(BF16)

    interleaved(work, count)


def hidden_kernel(
    step_count,
    core_ref,
    second_ref,
    cotangent_ref,
    up_weight_ref,
    down_weight_ref,
    up_bias_ref,
    grad_second_ref,
    down_send_ref,
    down_keep_ref,
    up_send_ref,
    up_keep_ref,
    bias_ref,
    hidden_ref,
    total_ref,
    second_turned_ref,
    grad_hidden_ref,
):
    step = pl.program_id(0)
    seq_count, tok_count, width = second_ref.shape

    @pl.when(step == 0)
    def _():
        total_ref[...] = jnp.zeros_like(total_ref)
        for at in range(seq_count):
            second_turned_ref[:, at * tok_count : (at + 1) * tok_count] = second_ref[at].T

    up_weight, down_weight = up_weight_ref[...], down_weight_ref[...]

    together = 2 - seq_count % 2
    block = together * tok_count

    def flat(ref, at):
        return ref[at * together : (at + 1) * together].reshape(block, width)

    def products(at):
        return (
            dot(flat(second_ref, at), up_weight),
            dot_nt(flat(cotangent_ref, at), down_weight),
        )

    up_bias = up_bias_ref[...]

    def bend(at, state):
        bias = 0.0
        for rows in tiles(block, TILE // 2):
            hidden_in = state[0][rows] + up_bias
            squares = hidden_in * hidden_in
            bent = jnp.tanh(hidden_in * (0.7978845608028654 + 0.035677408136300125 * squares))
            rising = 0.5 + 0.5 * bent
            slope = rising + hidden_in * (0.5 - 0.5 * bent * bent) * (
                0.7978845608028654 + 0.10703222440890037 * squares
            )
            grad_hidden = (state[1][rows] * slope).astype(BF16)
            places = slice(at * block + rows.start, at * block + rows.stop)
            hidden_ref[places, :] = (hidden_in * rising).astype(BF16)
            grad_hidden_ref[places, :] = grad_hidden
            bias = bias + partial_sum(grad_hidden.astype(F32))
        return bias

    def spread(at):
        rows = slice(at * block, (at + 1) * block)
        grads = dot_nt(grad_hidden_ref[rows, :], up_weight)
        for rows in tiles(block):
            sequence = at * together + rows.start // tok_count
            begin = rows.start % tok_count
            places = slice(begin, begin + TILE)
            total_ref[sequence, places] += grads[rows]

    state = products(0)
    bias = 0.0
    for at in range(seq_count // together):
        later = products(at + 1) if at + 1 < seq_count // together else None
        bias = bias + bend(at, state)
        spread(at)
        state = later
    bias_ref[...] = column_sum(bias)
    down = dot_tn(hidden_ref[...], cotangent_ref[...].reshape(seq_count * tok_count, width))
    up = dot(second_turned_ref[...], grad_hidden_ref[...]).reshape(up_send_ref.shape)

    @pl.when(step < step_count // 2)
    def _():
        down_send_ref[0] = down
        up_send_ref[...] = up

    @pl.when(step >= step_count // 2)
    def _():
        down_keep_ref[0] = down
        up_keep_ref[...] = up

    @pl.when(step == step_count - 1)
    def _():
        for at in range(seq_count):
            for rows in tiles(tok_count):
                grad_second_ref[at, rows] = total_ref[at, rows].astype(BF16)


def output_kernel(
    core_ref, hidden_ref, middle_ref, down_weight_ref, down_bias_ref, layer_ref
):
    results = dot(hidden_ref[...], down_weight_ref[...])
    bias = down_bias_ref[...]
    for rows in tiles(results.shape[0]):
        layer_ref[0, rows] = (middle_ref[0, rows] + results[rows] + bias).astype(BF16)


def backward_kernel(
    heights,
    shards,
    piece_count,
    lengths_ref,
    shard_ref,
    cotangent_ref,
    far_ref,
    middle_ref,
    outs_ref,
    level_ref,
    grad_second_ref,
    output_weight_ref,
    gain_ref,
    spread_ref,
    *refs,
):
    pieces = refs[:piece_count]
    refs = refs[piece_count + 2 :]
    grad_middle_ref, grad_attended_ref, inner_ref, grad_queries_ref = refs[:4]
    grad_pieces = refs[4 : piece_count + 4]
    send_ref, keep_ref, small_ref, weights_ref, project_ref, attended_ref = refs[piece_count + 4 :]
    step = pl.program_id(0)
    count, tok_count, width = middle_ref.shape

    @pl.when(step == 0)
    def _():
        weights_ref[...] = jnp.zeros_like(weights_ref)
        small_ref[...] = jnp.zeros_like(small_ref)

    gain = gain_ref[...]

    def work(own):
        far_keys, far_values, far_bias, inverse = far_state(
            step * count + own, lengths_ref, shard_ref[shard_ref.shape[0] - 1], tok_count, heights, shards, pieces
        )
        coarse = [far_ref[own, :, at * tok_count : (at + 1) * tok_count] for at in range(heights)]
        logits = [dot(far_keys[at], coarse[at]) for at in range(heights)]
        yield
        small = [0.0] * 4
        for rows in tiles(tok_count):
            normed, scale = normalize(middle_ref[own, rows])
            grad_second = grad_second_ref[own, rows].astype(F32)
            grad_result = cotangent_ref[own, rows].astype(F32)
            grad_middle = grad_result + normalize_back(grad_second * gain, normed, scale)
            grad_middle_ref[own, rows] = grad_middle
            grad_project = grad_middle.astype(BF16)
            project_ref[own, rows] = grad_project
            sums = [grad_result, grad_second * normed, grad_second, grad_project.astype(F32)]
            small = [total + partial_sum(part) for total, part in zip(small, sums)]
        for at, total in enumerate(small):
            small_ref[:, at * width : (at + 1) * width] += column_sum(total)
        grad_project = project_ref[own]
        yield
        grad_attended = dot_nt(output_weight_ref[...], grad_project)
        yield
        inners = []
        for head in range(HEADS):
            rows = slice(HALF * head, HALF * (head + 1))
            outs = outs_ref[own, rows, :]
            attended_ref[own, rows, :] = outs.astype(BF16)
            grads = grad_attended[rows].astype(BF16)
            grad_attended_ref[own, rows, :] = grads
            inners.append(column_sum(partial_sum(grads.astype(F32) * outs)))
            inner_ref[own, head : head + 1, :] = inners[-1]
        yield
        grad_attended = grad_attended_ref[own]
        add_to(weights_ref, dot(attended_ref[own], grad_project))
        grad_probs = dot(far_values, grad_attended)
        yield
        all_probs, all_grads = [], []
        for at in range(heights):
            probs_parts, grads_parts = [], []
            for head in range(HEADS):
                rows = slice(BLOCK * head, BLOCK * (head + 1))
                whole_rows = slice(HEADS * BLOCK * at + rows.start, HEADS * BLOCK * at + rows.stop)
                level = level_ref[own, head : head + 1, :]
                probs = jnp.exp(logits[at][rows] + far_bias[at] - level)
                probs_parts.append(probs.astype(BF16))
                grads_parts.append((probs * (grad_probs[whole_rows] - inners[head])).astype(BF16))
            all_probs.append(jnp.concatenate(probs_parts, axis=0))
            all_grads.append(jnp.concatenate(grads_parts, axis=0))
        yield
        all_spread = [dot(all_grads[at], spread_ref[at]).astype(BF16) for at in range(heights)]
        yield
        grad_queries = dot_tn(jnp.concatenate(far_keys, axis=0), jnp.concatenate(all_spread, axis=0))
        grad_queries_ref[own] = grad_queries.astype(BF16)
        wide_values = dot_nt(jnp.concatenate(all_probs, axis=0), grad_attended)
        yield
        grad_keys, grad_values = [], []
        for at in range(heights):
            rows = slice(HEADS * BLOCK * at, HEADS * BLOCK * (at + 1))
            grad_keys.append(of_heads(dot_nt(all_grads[at], coarse[at])))
            grad_values.append(of_heads(wide_values[rows]))
        grad_sums = jnp.concatenate(
            [
                jnp.concatenate(grad_keys, axis=0) * inverse,
                jnp.concatenate(grad_values, axis=0) * inverse,
            ],
            axis=1,
        )
        row = 0
        for piece in grad_pieces:
            rows = piece.shape[1]
            piece[own] = grad_sums[row : row + rows]
            row += rows

    interleaved(work, count)

    @pl.when(step == pl.num_programs(0) - 1)
    def _():
        split_rows(weights_ref, shard_ref[0], send_ref.at[0], keep_ref.at[0])


def near_back_kernel(
    begin,
    summing,
    lengths_ref,
    shard_ref,
    bits_ref,
    queries_ref,
    keys_ref,
    values_ref,
    grad_attended_ref,
    level_ref,
    inner_ref,
    spots_ref,
    spread_pair_ref,
    far_queries_ref,
    coarse_ref,
    pooled_keys_ref,
    pooled_values_ref,
    *refs,
):
    grad_queries_ref, grad_keys_ref, grad_values_ref, send_ref = refs[-4:]
    if summing:
        keep_ref, other_ref = refs[-6:-4]
        send_ref[...] = keep_ref[...] + other_ref[...]
    sequence = pl.program_id(0) + begin
    tok_count = keys_ref.shape[1]
    remaining = lengths_ref[sequence] - shard_ref[shard_ref.shape[0] - 1] * tok_count
    inverse = coarse_inverse(remaining)
    keys = chunk_keys(keys_ref[0], pooled_keys_ref[0])
    values = chunk_keys(values_ref[0], pooled_values_ref[0])
    queries = queries_ref[0]
    grad_attended = grad_attended_ref[0]
    bias = [local_bias(remaining, chunk) for chunk in range(2)]
    coarse = coarse_ref[0]
    levels = [level_queries(queries, coarse, chunk) for chunk in range(2)]
    grad_keys, grad_values = {}, {}

    def products(unit):
        chunk, pair = unit
        lanes = slice(chunk * CHUNK, (chunk + 1) * CHUNK)
        tall = [block_diagonal(part[pair_of(pair)]) for part in levels[chunk]]
        tall_grads = block_diagonal(grad_attended[pair_of(pair), lanes])
        logits = local_logits(keys[chunk], tall, pair)
        return tall[0], tall_grads, logits, dot(values[chunk][:, pair_of(pair)], tall_grads)

    def slopes(unit, state):
        chunk, pair = unit
        lanes = slice(chunk * CHUNK, (chunk + 1) * CHUNK)
        tall, tall_grads, logits, grad_probs = state
        probs_sides, grads_sides = [], []
        for side in range(2):
            half = slice(side * CHUNK, (side + 1) * CHUNK)
            head = 2 * pair + side
            level = level_ref[0, head : head + 1, lanes]
            inner = inner_ref[0, head : head + 1, lanes]
            probs_parts, grads_parts = [], []
            for at in range(4):
                for rows in tiles(LOCAL_ROWS[at], min(LOCAL_ROWS[at], 2 * TILE)):
                    begin = LOCAL_STARTS[at] + rows.start
                    probs = jnp.exp(logits[at][rows, half] + bias[chunk][at][rows] - level)
                    grads = grad_probs[begin : begin + rows.stop - rows.start, half]
                    probs_parts.append(probs.astype(BF16))
                    grads_parts.append((probs * (grads - inner)).astype(BF16))
            probs_sides.append(jnp.concatenate(probs_parts, axis=0))
            grads_sides.append(jnp.concatenate(grads_parts, axis=0))
        return (
            tall,
            tall_grads,
            jnp.concatenate(probs_sides, axis=1),
            jnp.concatenate(grads_sides, axis=1),
        )

    def grads(unit, state):
        tall, tall_grads, probs, grad_logits = state
        grad_values[unit] = dot_nt(probs, tall_grads)
        return tall, grad_logits

    held = skewed(products, slopes, grads)
    for chunk in range(2):
        lanes = slice(chunk * CHUNK, (chunk + 1) * CHUNK)
        pairs = range(HEADS // 2)
        spread = []
        for at in range(1, 4):
            begin, rows = LOCAL_STARTS[at], LOCAL_ROWS[at]
            parts = [held[chunk, pair][1][begin : begin + rows] for pair in pairs]
            spread.append(
                dot(jnp.concatenate(parts, axis=0), spread_pair_ref[at - 1]).astype(BF16)
            )
        for pair in pairs:
            tall, grad_logits = held[chunk, pair]
            parts = [grad_logits[:CHUNK]] + [
                spread[at - 1][pair * LOCAL_ROWS[at] : (pair + 1) * LOCAL_ROWS[at]]
                for at in range(1, 4)
            ]
            evened = jnp.concatenate(parts, axis=0)
            grad_keys[chunk, pair] = dot_nt(evened, tall)
            wide = dot_tn(keys[chunk][:, pair_of(pair)], evened)
            total = diagonal_blocks(wide) + far_queries_ref[0, pair_of(pair), lanes].astype(F32)
            grad_queries_ref[0, pair_of(pair), lanes] = (total * 0.125).astype(BF16)

    def gathered(parts, begin, end):
        return [
            jnp.concatenate([parts[chunk, pair][begin:end] for pair in range(HEADS // 2)], axis=1)
            for chunk in range(2)
        ]

    fine_keys, coarse_keys = gathered(grad_keys, 0, CHUNK), gathered(grad_keys, CHUNK, LOCAL_KEYS)
    fine_values = gathered(grad_values, 0, CHUNK)
    coarse_values = gathered(grad_values, CHUNK, LOCAL_KEYS)
    inverse = four_times(inverse)
    for out_ref, fine, coarse in (
        (grad_keys_ref, fine_keys, coarse_keys),
        (grad_values_ref, fine_values, coarse_values),
    ):
        pooled = (jnp.concatenate(coarse, axis=0) * inverse).astype(BF16)
        total = jnp.concatenate(fine, axis=0) + dot(spots_ref[...], pooled)
        out_ref[0] = total.astype(out_ref.dtype)


def last_kernel(
    heights,
    piece_heights,
    lengths_ref,
    shard_ref,
    tokens_ref,
    grad_middle_ref,
    grad_queries_ref,
    grad_keys_ref,
    grad_values_ref,
    query_weight_ref,
    key_weight_ref,
    value_weight_ref,
    gain_ref,
    shift_ref,
    groups_ref,
    grad_up_bias_ref,
    small_middle_ref,
    *refs,
):
    pieces = refs[: len(piece_heights)]
    input_grad_ref, send_ref, keep_ref, weights_ref, small_ref, normed_ref, grads_ref = refs[-7:]
    sequence = pl.program_id(0)
    count, tok_count, width = tokens_ref.shape

    @pl.when(sequence == 0)
    def _():
        weights_ref[...] = jnp.zeros_like(weights_ref)
        small_ref[0:1, :] = grad_up_bias_ref[...]
        small_ref[1:2, :] = small_middle_ref[...]
        small_ref[2:, :] = jnp.zeros((small_ref.shape[0] - 2, small_ref.shape[1]), F32)

    gain, shift = gain_ref[...], shift_ref[...]
    for at in range(count):
        remaining = lengths_ref[sequence * count + at] - shard_ref[shard_ref.shape[0] - 1] * tok_count
        far = [
            sum(piece[at] for piece, level in zip(pieces, piece_heights) if level == height)
            for height in range(heights)
        ]
        far = dot_tn(groups_ref[...], jnp.concatenate(far, axis=0).astype(BF16))
        grads_ref[at, :, :width] = grad_queries_ref[at].T
        for rows in tiles(tok_count):
            normed, _ = normalize(tokens_ref[at, rows].astype(F32))
            normed_ref[at, rows] = (normed * gain + shift).astype(BF16)
            valid = iota((TILE, width), 0) + rows.start < remaining
            keys = grad_keys_ref[at, rows].astype(F32) + far[rows, :width]
            values = grad_values_ref[at, rows].astype(F32) + far[rows, width:]
            keys = jnp.where(valid, keys, 0.0)
            values = jnp.where(valid, values, 0.0)
            grads_ref[at, rows, width : 2 * width] = keys.astype(BF16)
            grads_ref[at, rows, 2 * width :] = values.astype(BF16)
    grads = grads_ref[...].reshape(count * tok_count, 3 * width)
    grad_normed = (
        dot_nt(grads[:, :width], query_weight_ref[...])
        + dot_nt(grads[:, width : 2 * width], key_weight_ref[...])
        + dot_nt(grads[:, 2 * width :], value_weight_ref[...])
    )
    products = dot_tn(normed_ref[...].reshape(count * tok_count, width), grads)
    small = [0.0] * 4
    for at in range(count):
        for rows in tiles(tok_count):
            places = slice(at * tok_count + rows.start, at * tok_count + rows.stop)
            normed, scale = normalize(tokens_ref[at, rows].astype(F32))
            given = grad_normed[places]
            sums = [
                grads_ref[at, rows, :width].astype(F32),
                grads_ref[at, rows, 2 * width :].astype(F32),
                given * normed,
                given,
            ]
            small = [total + partial_sum(part) for total, part in zip(small, sums)]
            back = normalize_back(given * gain, normed, scale)
            input_grad_ref[at, rows] = grad_middle_ref[at, rows] + back
    for at, total in enumerate(small):
        small_ref[2:3, at * width : (at + 1) * width] += column_sum(total)
    for rows in tiles(width):
        weights_ref[rows, : 3 * width] += products[rows]

    @pl.when(sequence == pl.num_programs(0) - 1)
    def _():
        parts = small_ref.shape[1] // CHUNK
        for line in range(3):
            for part in range(parts):
                at = line * parts + part
                weights_ref[at : at + 1, 3 * width :] = small_ref[
                    line : line + 1, part * CHUNK : (part + 1) * CHUNK
                ]
        split_rows(weights_ref, shard_ref[0], send_ref.at[0], keep_ref.at[0])


def half_of(ref, bit):
    rows = ref.shape[1] // 2
    return ref[:, pl.ds(pl.multiple_of(bit * rows, 8), rows), :]


def first_sum_kernel(fetch, bits_ref, keep_ref, other_ref, token_ref, send_ref, next_ref, *scratch):
    rows = send_ref.shape[1]
    begin = pl.multiple_of((1 - bits_ref[1]) * rows, 8)
    fetched_ref, sems = scratch
    copies = []
    for at, ref in enumerate([keep_ref, other_ref][:fetch]):
        source = ref.at[:, pl.ds(begin, rows), :]
        copies.append(pltpu.make_async_copy(source, fetched_ref.at[at], sems.at[at]))
        copies[-1].start()
    for copy in copies:
        copy.wait()
    other = fetched_ref[1] if fetch > 1 else other_ref[:, pl.ds(begin, rows), :]
    send_ref[...] = fetched_ref[0] + other


def second_sum_kernel(
    fetch, bits_ref, keep_ref, other_ref, new_ref, token_ref, send_ref, stay_ref, next_ref, *scratch
):
    rows = new_ref.shape[1]
    half = rows // 2
    begin = pl.multiple_of(bits_ref[1] * rows, 8)
    fetched_ref, sems = scratch
    copies = []
    for at, ref in enumerate([keep_ref, other_ref][:fetch]):
        source = ref.at[:, pl.ds(begin, rows), :]
        copies.append(pltpu.make_async_copy(source, fetched_ref.at[at], sems.at[at]))
        copies[-1].start()
    for copy in copies:
        copy.wait()
    for out_ref, bit in ((send_ref, 1 - bits_ref[2]), (stay_ref, bits_ref[2])):
        offset = pl.multiple_of(bit * half, 8)
        part = pl.ds(offset, half)
        if fetch > 1:
            other = fetched_ref[1, :, part, :]
        else:
            other = other_ref[:, pl.ds(pl.multiple_of(begin + offset, 8), half), :]
        out_ref[...] = fetched_ref[0, :, part, :] + other + new_ref[:, part, :]


def split_sum_kernel(
    step, bits_ref, keep_ref, new_ref, token_ref, send_ref, stay_ref, next_ref
):
    bit = bits_ref[step]
    send_ref[...] = half_of(keep_ref, 1 - bit) + half_of(new_ref, 1 - bit)
    stay_ref[...] = half_of(keep_ref, bit) + half_of(new_ref, bit)


def last_sum_kernel(bits_ref, keep_ref, new_ref, token_ref, out_ref, next_ref):
    out_ref[...] = keep_ref[...] + new_ref[...]


def join_rows_kernel(step, bits_ref, own_ref, other_ref, token_ref, out_ref, next_ref):
    rows = own_ref.shape[1]
    bit = bits_ref[step]
    out_ref[:, pl.ds(pl.multiple_of(bit * rows, 8), rows), :] = own_ref[...]
    out_ref[:, pl.ds(pl.multiple_of((1 - bit) * rows, 8), rows), :] = other_ref[...]


def place_down_kernel(bits_ref, own_ref, other_ref, token_ref, out_ref, next_ref):
    rows = own_ref.shape[1]
    core = bits_ref[0]
    out_ref[pl.ds(pl.multiple_of(core * rows, 8), rows), :] = own_ref[0]
    out_ref[pl.ds(pl.multiple_of((1 - core) * rows, 8), rows), :] = other_ref[0]


def place_up_kernel(bits_ref, own_ref, other_ref, token_ref, up_ref, output_ref, next_ref):
    parts, rows, width = own_ref.shape
    core = bits_ref[0]
    for side in range(2):

        @pl.when(core == side)
        def _():
            for half, source in ((side, own_ref), (1 - side, other_ref)):
                for part in range(parts - 1):
                    column = (half * (parts - 1) // 2 + part // 2) * width
                    row = part % 2 * rows
                    up_ref[row : row + rows, column : column + width] = source[part]
                output_ref[half * rows : (half + 1) * rows, :] = source[parts - 1]


def place_last_kernel(vectors, bits_ref, own_ref, other_ref, token_ref, *refs):
    rows = own_ref.shape[1]
    core = bits_ref[0]
    outs, extra_ref = refs[:3], refs[-1]
    for half, source in ((core, own_ref), (1 - core, other_ref)):
        begin = pl.multiple_of(half * rows, 8)
        width = outs[0].shape[1]
        for at, out in enumerate(outs):
            out[pl.ds(begin, rows), :] = source[0, :, at * width : (at + 1) * width]
        extra_ref[pl.ds(begin, rows), :] = source[0, :, 3 * width :]
    row = 0
    for out in refs[3:-2]:
        for part in range(out.shape[1] // CHUNK):
            out[:, part * CHUNK : (part + 1) * CHUNK] = extra_ref[row : row + 1, :]
            row += 1


class Reducer:
    def __init__(self):
        self.shards = lax.axis_size("seq")
        self.batches = lax.axis_size("batch")
        seq_bits = self.shards.bit_length() - 1
        far_bits = self.batches.bit_length() - 2
        seq_half, far_half = seq_bits // 2, far_bits // 2
        orders = (
            [("seq", bit) for bit in range(seq_bits)]
            + [("batch", bit + 1) for bit in range(far_bits)],
            [("seq", (bit + seq_half) % seq_bits) for bit in range(seq_bits)]
            + [("batch", (bit + far_half) % far_bits + 1) for bit in range(far_bits)],
        )
        places = dict(seq=lax.axis_index("seq"), batch=lax.axis_index("batch"))
        core = places["batch"] & 1
        bits = [core]
        for first, second in zip(*orders):
            one, other = [(places[axis] >> bit) & 1 for axis, bit in (first, second)]
            bits.append(jnp.where(core == 0, one, other))
        self.steps = len(bits)
        self.token = None
        self.bits = jnp.stack(bits + [places["seq"]]).astype(jnp.int32)
        self.pairs = [[] for _ in range(self.steps)]
        for seq in range(self.shards):
            for batch in range(self.batches):
                moves = [("batch", 0)] + orders[batch & 1]
                for pairs, (axis, bit) in zip(self.pairs, moves):
                    to_seq = seq ^ (1 << bit) if axis == "seq" else seq
                    to_batch = batch ^ (1 << bit) if axis == "batch" else batch
                    pairs.append((seq * self.batches + batch, to_seq * self.batches + to_batch))

    def swap(self, array, step):
        return lax.ppermute(array, ("seq", "batch"), self.pairs[step])

    def run(self, kernel, name, in_specs, operands, out_specs, shapes, scratch=(), chunk=None, limit=32 * 2**20):
        anywhere = pl.BlockSpec(memory_space=pl.ANY)
        *outs, self.token = pl.pallas_call(
            kernel,
            in_specs=[pl.BlockSpec(memory_space=pltpu.SMEM)] + in_specs + [anywhere],
            out_specs=out_specs + [anywhere],
            out_shape=[jax.ShapeDtypeStruct(shape, F32) for shape in shapes + [TOKEN]],
            scratch_shapes=scratch,
            compiler_params=pltpu.CompilerParams(vmem_limit_bytes=limit),
            cost_estimate=pl.CostEstimate(
                flops=0, bytes_accessed=ROUND_BYTES[chunk], transcendentals=0
            ),
            name=name,
        )(self.bits, *operands, self.token)
        return outs

    def gate(self, name, *arrays):
        anywhere = pl.BlockSpec(memory_space=pl.ANY)
        *arrays, self.token = pl.pallas_call(
            lambda *refs: None,
            in_specs=[anywhere] * (len(arrays) + 1),
            out_specs=[anywhere] * (len(arrays) + 1),
            out_shape=[
                jax.ShapeDtypeStruct(shape, F32)
                for shape in [array.shape for array in arrays] + [TOKEN]
            ],
            input_output_aliases={at: at for at in range(len(arrays))},
            cost_estimate=pl.CostEstimate(flops=0, bytes_accessed=0, transcendentals=0),
            name=f"{name}_gate",
        )(*arrays, self.token)
        return arrays

    def total(self, name, terms, step, fetch):
        parts, full, width = terms[0].shape
        anywhere, vmem = pl.BlockSpec(memory_space=pl.ANY), pl.BlockSpec(memory_space=pltpu.VMEM)
        given = [anywhere] * fetch + [vmem] * (2 - fetch)
        if step <= 2:
            scratch = [
                pltpu.VMEM((fetch, parts, full // 2, width), F32),
                pltpu.SemaphoreType.DMA((fetch,)),
            ]
        if step == 1:
            kernel = functools.partial(first_sum_kernel, fetch)
            shapes = [(parts, full // 2, width)]
            (send,) = self.run(
                kernel, f"{name}_sum1", given, terms, [vmem], shapes, scratch, chunk=name
            )
            return send, terms
        if step == 2:
            kernel = functools.partial(second_sum_kernel, fetch)
            shapes = [(parts, full // 4, width)] * 2
            send, stay = self.run(
                kernel,
                f"{name}_sum2",
                given + [vmem],
                terms,
                [vmem] * 2,
                shapes,
                scratch,
                chunk=name,
                limit=VMEM_BYTES if fetch > 1 else 32 * 2**20,
            )
            return send, [stay]
        kernel = functools.partial(split_sum_kernel, step)
        shapes = [(parts, full // 2, width)] * 2
        send, stay = self.run(
            kernel, f"{name}_sum{step}", [vmem] * 2, terms, [vmem] * 2, shapes, chunk=name
        )
        return send, [stay]

    def finish(self, name, terms):
        vmem = pl.BlockSpec(memory_space=pltpu.VMEM)
        (out,) = self.run(
            last_sum_kernel, f"{name}_total", [vmem] * 2, terms, [vmem], [terms[0].shape], chunk=name
        )
        return out

    def join(self, name, own, other, step):
        parts, rows, width = own.shape
        vmem = pl.BlockSpec(memory_space=pltpu.VMEM)
        (out,) = self.run(
            functools.partial(join_rows_kernel, step),
            f"{name}_join{step}",
            [vmem, vmem],
            [own, other],
            [vmem],
            [(parts, 2 * rows, width)],
            chunk=name,
        )
        return out

    def place(self, name, kernel, own, other, shapes, scratch=()):
        vmem = pl.BlockSpec(memory_space=pltpu.VMEM)
        return self.run(
            kernel,
            f"{name}_place",
            [vmem, vmem],
            [own, other],
            [vmem] * len(shapes),
            shapes,
            scratch,
            chunk=name,
        )


class Chunk:
    def __init__(
        self,
        reducer,
        name,
        send,
        keep,
        kernel,
        shapes,
        scratch=(),
        gated=False,
        fetch=2,
    ):
        self.reducer, self.name = reducer, name
        self.last = reducer.steps - 1
        self.fits = keep.shape[1] >> self.last >= 8
        self.send, self.terms, self.gated, self.fetch = send, [keep], gated, fetch
        self.kernel, self.shapes, self.scratch = kernel, list(shapes), scratch
        self.outs = self.ready = None
        self.stages = self.run()

    def run(self):
        reducer, name, last = self.reducer, self.name, self.last
        if not self.fits:
            outs = reducer.place(
                name, self.kernel, self.terms[0], self.send, self.shapes, self.scratch
            )
            self.outs = lax.psum(outs, ("seq", "batch"))
            return
        if self.gated:
            (self.send,) = reducer.gate(name, self.send)
        self.terms = terms = self.terms + [reducer.swap(self.send, 0)]
        for step in range(1, last + 1):
            yield
            if step == 1 and self.ready is not None:
                send = self.ready
                if name == "down":
                    (send,) = reducer.gate(name, send)
            else:
                send, terms = reducer.total(name, terms, step, self.fetch)
            terms = terms + [reducer.swap(send, step)]
        yield
        block = reducer.finish(name, terms)
        for step in range(last, 0, -1):
            other = reducer.swap(block, step)
            yield
            block = reducer.join(name, block, other, step)
        other = reducer.swap(block, 0)
        yield
        self.outs = reducer.place(name, self.kernel, block, other, self.shapes, self.scratch)

    def first_sum(self, cuts):
        if not self.fits:
            return [], [], [pl.BlockSpec(TOKEN, lambda at, *_: (0, 0))], [(TOKEN, F32)]
        parts, full, width = self.terms[0].shape
        rows = full // 2
        block = (parts, rows // cuts, width)
        given = pl.BlockSpec(block, lambda at, *scalars: (0, (1 - scalars[2][1]) * cuts + at, 0))
        made = pl.BlockSpec(block, lambda at, *_: (0, at, 0))
        return self.terms, [given] * 2, [made], [((parts, rows, width), F32)]

    def forward(self):
        return next(self.stages, self) is not self


def by_sequence(*shape, begin=0, count=1):
    return pl.BlockSpec((count,) + shape, lambda at, *_: (at + begin,) + (0,) * len(shape))


def whole(*shape):
    return pl.BlockSpec(shape, lambda at, *_: (0,) * len(shape))


def call(
    reducer,
    kernel,
    grid,
    in_specs,
    out_specs,
    out_shapes,
    flops,
    operands,
    aliases=None,
    scratch=(),
    prefetch=2,
):
    anywhere = pl.BlockSpec(memory_space=pl.ANY)
    given, made = len(in_specs), len(out_specs)
    tokens = [] if reducer.token is None else [reducer.token]

    def body(*refs):
        inputs = refs[: prefetch + given]
        rest = refs[prefetch + given + len(tokens) :]
        kernel(*inputs, *rest[:made], *rest[made + 1 :])

    *outs, reducer.token = pl.pallas_call(
        body,
        grid_spec=pltpu.PrefetchScalarGridSpec(
            num_scalar_prefetch=prefetch,
            grid=grid,
            in_specs=in_specs + [anywhere] * len(tokens),
            out_specs=out_specs + [anywhere],
            scratch_shapes=scratch,
        ),
        out_shape=[
            jax.ShapeDtypeStruct(shape, dtype) for shape, dtype in out_shapes + [(TOKEN, F32)]
        ],
        input_output_aliases=aliases or {},
        compiler_params=pltpu.CompilerParams(
            dimension_semantics=("arbitrary",), vmem_limit_bytes=VMEM_BYTES
        ),
        cost_estimate=pl.CostEstimate(flops=flops, bytes_accessed=20_000_000, transcendentals=0),
    )(*operands, *tokens)
    return outs


def local(
    tokens,
    lengths,
    query_weight,
    key_weight,
    value_weight,
    output_weight,
    up_weight,
    down_weight,
    query_bias,
    value_bias,
    output_bias,
    up_bias,
    down_bias,
    first_gain,
    first_shift,
    second_gain,
    second_shift,
    cotangent,
):
    seq_count, tok_count, width = tokens.shape
    inner_width = up_weight.shape[1]
    shards = lax.axis_size("seq")
    heights = shards.bit_length() - 1
    grid = (seq_count,)
    reducer = Reducer()
    core = shard = reducer.bits

    def row(vector):
        return vector.reshape(1, -1)

    groups = []
    for height in range(heights):
        members = group_members(tok_count, BLOCK << height)
        groups.append(np.pad(members, ((0, max(8 - members.shape[0], 0)), (0, 0))))
    groups = jnp.asarray(np.concatenate(groups, axis=0), BF16)
    members = jnp.asarray(coarse_members(tok_count), BF16)
    spots = jnp.asarray(coarse_members(tok_count).T, BF16)
    near_spread = jnp.asarray(np.concatenate([averaging(at) for at in range(1, 4)], axis=1), BF16)
    near_pair = jnp.asarray(np.stack([averaging_pair(at) for at in range(1, 4)]), BF16)
    far_pair = jnp.asarray(np.stack([averaging_pair(4 + at) for at in range(heights)]), BF16)

    fine = by_sequence(tok_count, width)
    tall = by_sequence(width, tok_count)
    heads = by_sequence(HEADS, tok_count)
    square = whole(width, width)
    vector = whole(1, width)
    fine_shape = (seq_count, tok_count, width)
    tall_shape = (seq_count, width, tok_count)
    heads_shape = (seq_count, HEADS, tok_count)
    sum_shapes = [(BLOCK >> height, 2 * width) for height in range(heights)]
    together = 2 - seq_count % 2
    some_fine = by_sequence(tok_count, width, count=together)
    some_tall = by_sequence(width, tok_count, count=together)
    queries, keys, values, *sums = call(
        reducer,
        functools.partial(project_kernel, heights),
        (seq_count // together,),
        [some_fine, square, square, square, vector, vector, vector, vector, whole(*groups.shape)],
        [some_tall, some_fine, some_fine]
        + [by_sequence(*shape, count=together) for shape in sum_shapes],
        [(tall_shape, BF16), (fine_shape, BF16), (fine_shape, BF16)]
        + [((seq_count,) + shape, F32) for shape in sum_shapes],
        2 * seq_count * tok_count * width * width * 3,
        scratch=[pltpu.VMEM((together, tok_count, width), BF16)] * 2,
        operands=[lengths,
        shard,
        tokens,
        query_weight,
        key_weight,
        value_weight,
        row(query_bias),
        row(value_bias),
        row(first_gain),
        row(first_shift),
        groups],
    )

    def swap(array, mask):
        return lax.ppermute(array, "seq", [(at, at ^ mask) for at in range(shards)])

    received = [swap(sums[mask.bit_length() - 1], mask) for mask in range(1, shards)]
    pieces = received[:3]
    for height in range(2, heights):
        pieces.append(
            jnp.concatenate(received[(1 << height) - 1 : (2 << height) - 1], axis=1)
        )
    piece_shapes = [piece.shape[1:] for piece in pieces]
    piece_specs = [by_sequence(*shape, count=together) for shape in piece_shapes]

    spread_shape = (seq_count, width, 2 * near_spread.shape[1])
    pool_shape = (seq_count, members.shape[0], width)
    spread_block, pool_block = by_sequence(*spread_shape[1:]), by_sequence(*pool_shape[1:])
    maxima, totals, numer, near_queries, pooled_near_keys, pooled_near_values = call(
        reducer,
        near_kernel,
        grid,
        [tall, fine, fine, whole(*members.shape), whole(*near_spread.shape)],
        [heads, heads, tall, spread_block, pool_block, pool_block],
        [
            (heads_shape, F32),
            (heads_shape, F32),
            (tall_shape, BF16),
            (spread_shape, BF16),
            (pool_shape, BF16),
            (pool_shape, BF16),
        ],
        1_000_000_000,
        [lengths, shard, queries, keys, values, members, near_spread],
    )

    some_heads = by_sequence(HEADS, tok_count, count=together)
    middle, second, outs, level, all_far_queries = call(
        reducer,
        functools.partial(join_kernel, heights, shards, len(pieces)),
        (seq_count // together,),
        [
            some_fine,
            some_tall,
            some_heads,
            some_heads,
            some_tall,
            square,
            vector,
            vector,
            vector,
            whole(*far_pair.shape),
        ]
        + [pl.BlockSpec(memory_space=pltpu.VMEM)] * len(pieces),
        [some_fine, some_fine, some_tall, some_heads]
        + [by_sequence(width, heights * tok_count, count=together)],
        [
            (fine_shape, F32),
            (fine_shape, BF16),
            (tall_shape, F32),
            (heads_shape, F32),
            ((seq_count, width, heights * tok_count), BF16),
        ],
        2 * seq_count * tok_count * width * width,
        scratch=[pltpu.VMEM((together, width, tok_count), BF16)],
        operands=[lengths,
        shard,
        tokens,
        queries,
        maxima,
        totals,
        numer,
        output_weight,
        row(output_bias),
        row(second_gain),
        row(second_shift),
        far_pair,
        *pieces],
    )

    steps = inner_width // width
    half_steps = steps // 2
    all_rows = whole(*fine_shape)

    def turned(at, core):
        return lax.rem(at + half_steps * (1 - core[0]), steps)

    columns = pl.BlockSpec((width, width), lambda at, core: (0, turned(at, core)))
    column_row = pl.BlockSpec((1, width), lambda at, core: (0, turned(at, core)))
    blocks = pl.BlockSpec((width, width), lambda at, core: (turned(at, core), 0))
    rows_count = seq_count * tok_count
    half_width = width // 2
    parts = steps + 1

    def halves(block, axis):
        def place(at):
            return tuple(at if place == axis else 0 for place in range(3))

        return [
            pl.BlockSpec(block, lambda at, core: place(jnp.minimum(at, half_steps - 1))),
            pl.BlockSpec(block, lambda at, core: place(jnp.maximum(at - half_steps, 0))),
        ]

    grad_second, down_send, down_keep, up_send, up_keep, grad_up_bias, hidden = call(
        reducer,
        functools.partial(hidden_kernel, steps),
        (steps,),
        [all_rows, all_rows, columns, blocks, column_row],
        [all_rows]
        + halves((1, width, width), 1)
        + halves((2, half_width, width), 0)
        + [column_row, pl.BlockSpec((rows_count, width), lambda at, core: (0, turned(at, core)))],
        [
            (fine_shape, BF16),
            ((1, inner_width // 2, width), F32),
            ((1, inner_width // 2, width), F32),
            ((parts, half_width, width), F32),
            ((parts, half_width, width), F32),
            ((1, inner_width), F32),
            ((rows_count, inner_width), BF16),
        ],
        2 * rows_count * width * 5 * inner_width,
        [core, second, cotangent, up_weight, down_weight, row(up_bias)],
        scratch=[
            pltpu.VMEM(fine_shape, F32),
            pltpu.VMEM((width, rows_count), BF16),
            pltpu.VMEM((rows_count, width), BF16),
        ],
        prefetch=1,
    )
    chunk_down = Chunk(
        reducer,
        "down",
        down_send,
        down_keep,
        place_down_kernel,
        [(inner_width, width)],
    )
    chunk_down.forward()

    grad_middle, grad_attended, inner_sums, far_queries, *rest = call(
        reducer,
        functools.partial(backward_kernel, heights, shards, len(pieces)),
        (seq_count // together,),
        [
            some_fine,
            by_sequence(width, heights * tok_count, count=together),
            some_fine,
            some_tall,
            some_heads,
            some_fine,
            square,
            vector,
            whole(*far_pair.shape),
        ]
        + [pl.BlockSpec(memory_space=pltpu.VMEM)] * len(pieces)
        + [pl.BlockSpec(memory_space=pl.ANY)] * 2,
        [some_fine, some_tall, some_heads, some_tall]
        + piece_specs
        + [pl.BlockSpec((1, half_width, width), lambda at, *_: (parts - 1, 0, 0))] * 2
        + [whole(1, inner_width)],
        [
            (fine_shape, F32),
            (tall_shape, BF16),
            (heads_shape, F32),
            (tall_shape, BF16),
        ]
        + [((seq_count,) + shape, F32) for shape in piece_shapes]
        + [((parts, half_width, width), F32)] * 2
        + [((1, inner_width), F32)],
        2 * rows_count * width * 2 * width,
        [lengths,
        shard,
        cotangent,
        all_far_queries,
        middle,
        outs,
        level,
        grad_second,
        output_weight,
        row(second_gain),
        far_pair,
        *pieces,
        up_send,
        up_keep],
        aliases={
            11 + len(pieces): 4 + len(pieces),
            12 + len(pieces): 5 + len(pieces),
        },
        scratch=[
            pltpu.VMEM((width, width), F32),
            pltpu.VMEM((together, tok_count, width), BF16),
            pltpu.VMEM((together, width, tok_count), BF16),
        ],
    )
    grad_pieces = rest[: len(pieces)]
    up_send, up_keep, small_middle = rest[len(pieces) :]
    chunk_up = Chunk(
        reducer,
        "up",
        up_send,
        up_keep,
        place_up_kernel,
        [(width, inner_width), (width, width)],
    )
    turns, layer = dict(d=chunk_down, u=chunk_up), []

    def take(place):
        for turn in ROUNDS.split(",")[place]:
            if turn == "o":
                layer.extend(
                    call(
                        reducer,
                        output_kernel,
                        grid,
                        [
                            pl.BlockSpec((tok_count, inner_width), lambda at, *_: (at, 0)),
                            fine,
                            whole(inner_width, width),
                            vector,
                        ],
                        [fine],
                        [(fine_shape, BF16)],
                        2 * rows_count * width * inner_width,
                        [core, hidden, middle, down_weight, row(down_bias)],
                        prefetch=1,
                    )
                )
            else:
                turns[turn].forward()

    returned = []
    for mask in range(1, shards):
        height = mask.bit_length() - 1
        if height < 2:
            piece = grad_pieces[mask - 1]
        else:
            rows = BLOCK >> height
            begin = (mask - (1 << height)) * rows
            piece = grad_pieces[height + 1][:, begin : begin + rows]
        returned.append(swap(piece, mask))
    take(0)
    half = seq_count // 2
    near_grads = ()
    anywhere = pl.BlockSpec(memory_space=pl.ANY)
    for begin in (0, half):
        some = functools.partial(by_sequence, begin=begin)
        some_fine, some_tall = some(tok_count, width), some(width, tok_count)
        some_heads = some(HEADS, tok_count)
        in_specs = [
            some_tall,
            some_fine,
            some_fine,
            some_tall,
            some_heads,
            some_heads,
            whole(*spots.shape),
            whole(*near_pair.shape),
            some_tall,
            some(*spread_shape[1:]),
            some(*pool_shape[1:]),
            some(*pool_shape[1:]),
        ]
        chunk = chunk_up if begin else chunk_down
        terms, sum_in, sum_out, sum_shape = chunk.first_sum(half)
        *near_grads, send = call(
            reducer,
            functools.partial(near_back_kernel, begin, len(terms) > 0),
            (half,),
            in_specs + [anywhere] * len(near_grads) + sum_in,
            [some_tall, some_fine, some_fine] + sum_out,
            [(tall_shape, BF16), (fine_shape, F32), (fine_shape, BF16)] + sum_shape,
            2_000_000_000,
            [
                lengths,
                shard,
                reducer.bits,
                queries,
                keys,
                values,
                grad_attended,
                level,
                inner_sums,
                spots,
                near_pair,
                far_queries,
                near_queries,
                pooled_near_keys,
                pooled_near_values,
                *near_grads,
                *terms,
            ],
            {3 + len(in_specs) + at: at for at in range(len(near_grads))},
            prefetch=3,
        )
        chunk.ready = send
        if begin == 0:
            returned = reducer.gate("far", *returned)
            take(1)
    take(2)

    back_pieces, back_heights = [], []
    for mask in range(1, shards):
        height = mask.bit_length() - 1
        if height < 2:
            back_pieces.append(returned[mask - 1])
            back_heights.append(height)
    for height in range(2, heights):
        total = sum(returned[(1 << height) - 1 : (2 << height) - 1])
        back_pieces.append(jnp.pad(total, ((0, 0), (0, 8 - total.shape[1]), (0, 0))))
        back_heights.append(height)
    some_fine = by_sequence(tok_count, width, count=together)
    some_tall = by_sequence(width, tok_count, count=together)
    input_grad, last_send, last_keep = call(
        reducer,
        functools.partial(last_kernel, heights, tuple(back_heights)),
        (seq_count // together,),
        [
            some_fine,
            some_fine,
            some_tall,
            some_fine,
            some_fine,
            square,
            square,
            square,
            vector,
            vector,
            whole(*groups.shape),
            whole(1, inner_width),
            whole(1, inner_width),
        ]
        + [by_sequence(*piece.shape[1:], count=together) for piece in back_pieces],
        [some_fine] + [whole(1, half_width, 3 * width + CHUNK)] * 2,
        [(fine_shape, F32)] + [((1, half_width, 3 * width + CHUNK), F32)] * 2,
        2 * seq_count * tok_count * width * width * 6,
        [lengths,
        shard,
        tokens,
        grad_middle,
        *near_grads,
        query_weight,
        key_weight,
        value_weight,
        row(first_gain),
        row(first_shift),
        groups,
        grad_up_bias,
        small_middle,
        *back_pieces],
        scratch=[
            pltpu.VMEM((width, 3 * width + CHUNK), F32),
            pltpu.VMEM((8, inner_width), F32),
            pltpu.VMEM((together, tok_count, width), BF16),
            pltpu.VMEM((together, tok_count, 3 * width), BF16),
        ],
    )
    vectors = [inner_width] + [width] * 8
    chunk_last = Chunk(
        reducer,
        "last",
        last_send,
        last_keep,
        functools.partial(place_last_kernel, vectors),
        [(width, width)] * 3 + [(1, length) for length in vectors],
        [pltpu.VMEM((width, CHUNK), F32)],
        gated=True,
        fetch=1,
    )
    turns["l"] = chunk_last
    take(3)
    for chunk in turns.values():
        while chunk.forward():
            pass
    grad_query, grad_key, grad_value, *vectors = chunk_last.outs
    (grad_down,) = chunk_down.outs
    grad_up, grad_output = chunk_up.outs
    (
        grad_up_bias,
        grad_down_bias,
        grad_second_gain,
        grad_second_shift,
        grad_output_bias,
        grad_query_bias,
        grad_value_bias,
        grad_first_gain,
        grad_first_shift,
    ) = [vector.reshape(-1) for vector in vectors]
    return (
        layer[0],
        input_grad,
        grad_query,
        grad_key,
        grad_value,
        grad_output,
        grad_up,
        grad_down,
        grad_query_bias,
        grad_value_bias,
        grad_output_bias,
        grad_up_bias,
        grad_down_bias,
        grad_first_gain,
        grad_first_shift,
        grad_second_gain,
        grad_second_shift,
    )


def solution(mesh):
    rows = P("batch", "seq", None)
    return jax.shard_map(
        local,
        mesh=mesh,
        in_specs=(rows, P("batch")) + (P(),) * 15 + (rows,),
        out_specs=(rows, rows) + (P(),) * 15,
        check_vma=False,
    )
```
